128 devices in a mesh: kx: 16 (over z, x_lo, core), ky: 8 (over y, x_hi).
Axes of the slice: x: 4 (x_hi: 2, x_lo: 2; x = x_hi * 2 + x_lo), y: 4, z: 4, core: 2. Of those that a mesh axis runs over, the one named last changes fastest.
Arguments:
- crossed: bfloat16 [2, 80, 80, 6400], P(None, 'kx', 'ky'), may hold values from -6 to 6
- vertex: bfloat16 [80, 80, 6400], P('kx', 'ky'), may hold values from -0.625 to 0.625
- bubble: bfloat16 [80, 80, 16, 5, 5], P('kx', 'ky'), may hold values from -3 to 3
- pair_map: int32 [2, 25], replicated, may hold values from 0 to 24, each once within a row
- bond_shift: int32 [2, 5, 5, 2], replicated, may hold values from -2 to 2
- envelope: float32 [2, 80, 80], replicated, may hold values from 0.25 to 4
Outputs:
- correction: bfloat16 [80, 80, 6400], P('kx', 'ky')
The draws below stay inside these ranges and needn't reach their ends.
Inputs may be any that keep to these rules, and one draw needn't show every extreme that they name: `pair_map`: each row names every form-factor pair once.
All inputs are finite; a program needn't handle non-finite values.
Results may differ from the reference program's by a relative error of at most 0.0095.
Values may be sent and summed in bfloat16 or wider, within the bound.
A program may use at most 64 MiB of HBM per device.

```python
import math
import jax
import jax.numpy as jnp
from jax import lax

LAT = 80
NFF = 5
NFREQ = 16
CHANNELS = 2
ORDER = 80


def touch_ends(entries, key, low, high):
    longest = entries.shape.index(max(entries.shape))
    spots = []
    for shift in (0, 1):
        where = [jax.random.randint(jax.random.fold_in(key, axis), (), 0, length) for axis, length in enumerate(entries.shape)]
        where[longest] = (where[longest] + shift) % entries.shape[longest]
        spots.append(tuple(where))
    return entries.at[spots[0]].set(low).at[spots[1]].set(high)


def level_of(key, dims, cuts, low, top_value):
    factor_of, own = 1.0, jax.random.fold_in(key, 6)
    for axis_at, shards_of in cuts:
        heights = jnp.exp(jax.random.uniform(jax.random.fold_in(own, axis_at), (shards_of,), jnp.float32, low / len(cuts), top_value / len(cuts)))
        factor_of = factor_of * jnp.repeat(heights, dims[axis_at] // shards_of).reshape([-1 if axis == axis_at else 1 for axis in range(len(dims))])
    return factor_of


def scatter_about(own_key, extent, deviation, bound, shards=(), held_as=jnp.bfloat16):
    array = jax.random.normal(own_key, extent, jnp.float32) * deviation
    if len(shards) > 0:
        array = level_of(own_key, extent, shards, -0.22, 0.18) * array
    return jnp.clip(array, min=-bound, max=bound).astype(held_as)


def setup_inputs(seed: int = 0) -> dict:
    key_of = jax.random.split(jax.random.key(seed), 7)
    return {
        "crossed": scatter_about(key_of[0], (CHANNELS, LAT, LAT, ORDER * ORDER), 1.0, 6.0, ((1, 16), (2, 8))),
        "vertex": scatter_about(key_of[1], (LAT, LAT, ORDER * ORDER), ORDER ** -0.5, 0.625, ((0, 16), (1, 8))),
        "bubble": scatter_about(key_of[2], (LAT, LAT, NFREQ, NFF, NFF), 0.45, 3.0, ((0, 16), (1, 8))),
        "pair_map": jax.vmap(lambda own: jax.random.permutation(own, NFF * NFF))(jax.random.split(key_of[3], CHANNELS)).reshape((CHANNELS, NFF * NFF)).astype(jnp.int32),
        "bond_shift": touch_ends(jax.random.randint(key_of[4], (CHANNELS, NFF, NFF, 2), -2, 3), jax.random.fold_in(key_of[4], 1), -2, 2).astype(jnp.int32),
        "envelope": jnp.clip(jnp.exp(jax.random.uniform(key_of[5], (CHANNELS, LAT, LAT), jnp.float32, math.log(0.25), math.log(4.0))), 0.25, 4.0),
    }


def cas_table(count):
    positions = jnp.arange(count, dtype=jnp.int32)
    phases = positions[:, None] * positions[None, :] % count
    angles = phases.astype(jnp.float32) * (2.0 * math.pi / count)
    return ((jnp.cos(angles) + jnp.sin(angles)) / math.sqrt(count)).astype(jnp.bfloat16)

def shifted(segment, step_x, step_y):
    count_x = segment.shape[0]
    count_y = segment.shape[1]
    rows_x = (jnp.arange(count_x, dtype=jnp.int32) + step_x) % count_x
    rows_y = (jnp.arange(count_y, dtype=jnp.int32) + step_y) % count_y
    return jnp.take(jnp.take(segment, rows_x, axis=0), rows_y, axis=1)

def project_pairs(real_space, pair_map, bond_shift, envelope):
    channels, count_x, count_y, blocks_a, form_count, blocks_b, _ = real_space.shape
    pair_rows = jnp.transpose(real_space, (0, 4, 6, 1, 2, 3, 5))
    pair_rows = pair_rows.reshape(channels, form_count * form_count, count_x, count_y, blocks_a, blocks_b)
    chosen = jax.vmap(lambda segment, mapping: jnp.take(segment, mapping, axis=0))(pair_rows, pair_map)
    shift_pairs = bond_shift.reshape(channels, form_count * form_count, 2)
    displaced = jax.vmap(jax.vmap(shifted))(chosen, shift_pairs[:, :, 0], shift_pairs[:, :, 1])
    weighted = displaced.astype(jnp.float32) * envelope[:, None, :, :, None, None]
    summed = lax.optimization_barrier(jnp.sum(weighted, axis=0)).astype(jnp.bfloat16)
    summed = summed.reshape(form_count, form_count, count_x, count_y, blocks_a, blocks_b)
    summed = jnp.transpose(summed, (2, 3, 4, 0, 5, 1))
    return summed.reshape(count_x, count_y, blocks_a * form_count, blocks_b * form_count)

def apply_bubble(bubble_row, matrix):
    blocked = matrix.reshape(matrix.shape[0], NFREQ, NFF, ORDER).astype(jnp.float32)
    product = jnp.einsum('ynab,ynbk->ynak', bubble_row.astype(jnp.float32), blocked, precision=lax.Precision.HIGHEST)
    return product.reshape(matrix.shape).astype(jnp.bfloat16)

def reference(crossed, vertex, bubble, pair_map, bond_shift, envelope):
    crossed = crossed.reshape(CHANNELS, LAT, LAT, ORDER, ORDER)
    vertex = vertex.reshape(LAT, LAT, ORDER, ORDER)
    cas_wide = cas_table(LAT).astype(jnp.float32)

    def one_frequency(frequency):
        start = (frequency * NFF).astype(jnp.int32)
        row_block = lax.dynamic_slice_in_dim(crossed, start, NFF, axis=3).astype(jnp.float32)
        half_done = jnp.einsum('ax,cxyrk->cayrk', cas_wide, row_block, precision=lax.Precision.HIGHEST).astype(jnp.bfloat16)
        real_space = jnp.einsum('by,cxyrk->cxbrk', cas_wide, half_done.astype(jnp.float32), precision=lax.Precision.HIGHEST).astype(jnp.bfloat16)
        real_space = real_space.reshape(CHANNELS, LAT, LAT, 1, NFF, NFREQ, NFF)
        projected_real = project_pairs(real_space, pair_map, bond_shift, envelope)
        back_half = jnp.einsum('by,xyrk->xbrk', cas_wide, projected_real.astype(jnp.float32), precision=lax.Precision.HIGHEST).astype(jnp.bfloat16)
        return jnp.einsum('ax,xyrk->ayrk', cas_wide, back_half.astype(jnp.float32), precision=lax.Precision.HIGHEST).astype(jnp.bfloat16)
    blocks = lax.map(one_frequency, jnp.arange(NFREQ, dtype=jnp.int32))
    projected = jnp.transpose(blocks, (1, 2, 0, 3, 4)).reshape(LAT, LAT, ORDER, ORDER)

    def one_row(operands):
        projected_row, vertex_row, bubble_row = operands
        left_factor = apply_bubble(bubble_row, vertex_row)
        right_factor = apply_bubble(bubble_row, projected_row)
        summed = jnp.einsum('yij,yjk->yik', projected_row.astype(jnp.float32), left_factor.astype(jnp.float32), precision=lax.Precision.HIGHEST)
        summed = summed + jnp.einsum('yij,yjk->yik', vertex_row.astype(jnp.float32), right_factor.astype(jnp.float32), precision=lax.Precision.HIGHEST)
        return summed.astype(jnp.bfloat16)
    result = lax.map(one_row, (projected, vertex, bubble))
    return result.reshape(LAT, LAT, ORDER * ORDER)
```

```python
import functools
import math

import jax
import jax.numpy as jnp
from jax import lax
from jax.experimental import pallas as pl
from jax.experimental.pallas import tpu as pltpu
from jax.sharding import PartitionSpec as P

LAT = 80
NFF = 5
NFREQ = 16
ORDER = 80
NX = 16
NY = 8
DEVICES = NX * NY
MESH = pl.DeviceIdType.MESH


def cas_table(count):
    positions = jnp.arange(count, dtype=jnp.int32)
    phases = positions[:, None] * positions[None, :] % count
    angles = phases.astype(jnp.float32) * (2.0 * math.pi / count)
    return ((jnp.cos(angles) + jnp.sin(angles)) / math.sqrt(count)).astype(jnp.bfloat16)


def exchange_kernel(send_ref, recv_ref, send_sem, recv_sems):
    mx = lax.axis_index("kx")
    my = lax.axis_index("ky")
    me = mx * NY + my
    barrier = pltpu.get_barrier_semaphore()

    def partner(step):
        other = lax.rem(me + lax.rem(step * 37, DEVICES), DEVICES)
        return other, (other // NY, lax.rem(other, NY))

    def greet(step, carry):
        _, where = partner(step)
        pl.semaphore_signal(barrier, inc=1, device_id=where, device_id_type=MESH)
        return carry

    lax.fori_loop(1, DEVICES, greet, 0)
    own = pltpu.make_async_copy(send_ref.at[me], recv_ref.at[me], recv_sems.at[mx])
    own.start()
    pl.semaphore_wait(barrier, DEVICES - 1)

    def send(step, carry):
        other, where = partner(step)
        pltpu.make_async_remote_copy(
            src_ref=send_ref.at[other],
            dst_ref=recv_ref.at[me],
            send_sem=send_sem,
            recv_sem=recv_sems.at[mx],
            device_id=where,
            device_id_type=MESH,
        ).start()
        return carry

    lax.fori_loop(1, DEVICES, send, 0)
    for group in range(NX):
        rows = pl.ds(NY * group, NY)
        pltpu.make_async_copy(send_ref.at[rows], recv_ref.at[rows], recv_sems.at[group]).wait()
    rows = pl.ds(0, DEVICES - 1)
    pltpu.make_async_copy(send_ref.at[rows], recv_ref.at[rows], send_sem).wait()


def exchange(slabs, collective_id):
    return pl.pallas_call(
        exchange_kernel,
        out_shape=jax.ShapeDtypeStruct(slabs.shape, slabs.dtype),
        in_specs=[pl.BlockSpec(memory_space=pltpu.VMEM)],
        out_specs=pl.BlockSpec(memory_space=pltpu.VMEM),
        scratch_shapes=[pltpu.SemaphoreType.DMA, pltpu.SemaphoreType.DMA((NX,))],
        compiler_params=pltpu.CompilerParams(
            collective_id=collective_id, has_side_effects=True, vmem_limit_bytes=32 * 2**20
        ),
    )(slabs)


def local(crossed, vertex, bubble, pair_map, bond_shift, envelope):
    f32 = jnp.float32
    bf16 = jnp.bfloat16
    cas = cas_table(LAT)
    slabs = crossed.reshape(2, 5, 10, 16, 5, 8, 2, 5).transpose(3, 5, 6, 2, 0, 1, 4, 7)
    slabs = jnp.pad(slabs.reshape(DEVICES, 40, 125), ((0, 0), (0, 0), (0, 3)))
    got = exchange(slabs, 0)[:, :, :125].reshape(16, 8, 2, 10, 2, 5, 25)
    got = got.transpose(4, 6, 2, 0, 5, 1, 3).reshape(2, 25, 2, 80, 80)
    shift = bond_shift.reshape(2, 25, 2)
    rows = (jnp.arange(LAT)[None, None, None, :] + shift[..., None]) % LAT
    cas_rows = jnp.take(cas, rows, axis=0)
    got = jnp.stack([jnp.take(got[c], pair_map[c], axis=0) for c in range(2)])
    half = jnp.einsum("cprx,cpnxy->cpnry", cas_rows[:, :, 0], got, preferred_element_type=f32).astype(bf16)
    real = jnp.einsum("cpsy,cpnry->cpnrs", cas_rows[:, :, 1], half, preferred_element_type=f32).astype(bf16)
    proj = jnp.sum(real.astype(f32) * envelope[:, None, None], axis=0).astype(bf16)
    back = jnp.einsum("ys,pnrs->pnry", cas, proj, preferred_element_type=f32).astype(bf16)
    back = jnp.einsum("xr,pnry->pnxy", cas, back, preferred_element_type=f32).astype(bf16)
    back = back.reshape(25, 2, 16, 5, 8, 10).transpose(2, 4, 1, 5, 3, 0).reshape(DEVICES, 20, 125)
    back = jnp.pad(back, ((0, 0), (0, 0), (0, 3)))
    got = exchange(back, 1)[:, :, :125].reshape(16, 8, 2, 10, 5, 5, 5)
    projected = got.transpose(4, 3, 0, 5, 1, 2, 6).reshape(5, 10, ORDER, ORDER)
    vertex = vertex.reshape(5, 10, ORDER, ORDER)

    def apply_bubble(matrix):
        blocked = matrix.reshape(5, 10, NFREQ, NFF, ORDER)
        product = jnp.einsum("xynab,xynbk->xynak", bubble, blocked, preferred_element_type=f32)
        return product.reshape(matrix.shape).astype(bf16)

    out = jnp.einsum("xyij,xyjk->xyik", projected, apply_bubble(vertex), preferred_element_type=f32)
    out = out + jnp.einsum("xyij,xyjk->xyik", vertex, apply_bubble(projected), preferred_element_type=f32)
    return out.astype(bf16).reshape(5, 10, ORDER * ORDER)


def solution(mesh):
    placed = (
        P(None, "kx", "ky", None),
        P("kx", "ky", None),
        P("kx", "ky", None, None, None),
        P(),
        P(),
        P(),
    )
    return jax.shard_map(
        local, mesh=mesh, in_specs=placed, out_specs=P("kx", "ky", None), check_vma=False
    )
```

```python
import math

import jax
import jax.numpy as jnp
import ml_dtypes
import numpy as np
from jax import lax
from jax.experimental import pallas as pl
from jax.experimental.pallas import tpu as pltpu
from jax.sharding import PartitionSpec as P

LAT = 80
NFF = 5
NFREQ = 16
ORDER = 80
NX = 16
NY = 8
DEVICES = NX * NY
QX = LAT // NX
QY = LAT // NY
REACH = 2
SEND_ROWS = 40
BACK_ROWS = 24
UNROLL = 5
BF16 = ml_dtypes.bfloat16
MESH = pl.DeviceIdType.MESH


def cas_table(count):
    phases = np.outer(np.arange(count), np.arange(count)) % count
    angles = phases * (2.0 * math.pi / count)
    return ((np.cos(angles) + np.sin(angles)) / math.sqrt(count)).astype(np.float32)


CAS = cas_table(LAT)


def rolled_rows():
    rows = (np.arange(LAT)[None, :] + np.arange(-REACH, REACH + 1)[:, None]) % LAT
    return CAS[rows].astype(BF16)


def y_forward():
    reach = np.zeros((LAT, 128), np.float32)
    columns = np.arange(LAT + 2 * REACH)
    reach[:, columns] = CAS[:, (columns - REACH) % LAT]
    reach = reach.reshape(NY, QY, 128)
    table = np.zeros((NY, 2, QY, 2, 2, 2, 128), np.float32)
    for chan in range(2):
        for half in range(2):
            table[:, half, :, chan, chan, half] = reach
    return table.reshape(NY * SEND_ROWS, 4 * 128).astype(BF16)


def x_back():
    table = np.zeros((NX, 8, LAT), np.float32)
    table[:, :QX] = CAS.reshape(NX, QX, LAT)
    return table.reshape(NX * 8, LAT).astype(BF16)


def y_back():
    table = np.zeros((NY, 2, 12, 2, 128), np.float32)
    for half in range(2):
        table[:, half, :QY, half, :LAT] = CAS.reshape(NY, QY, LAT)
    return table.reshape(NY * BACK_ROWS, 2 * 128).astype(BF16)


def main_kernel(
    pair_ref, shift_ref, slabs_ref, envelope_ref, cas_ref, yf_ref, xb_ref, yb_ref,
    out_ref, recv_ref, half_ref, back_ref, outgoing_ref,
    send_sem, recv_sems, back_send_sem, back_sems,
):
    mx = lax.axis_index("kx")
    my = lax.axis_index("ky")
    me = mx * NY + my
    barrier = pltpu.get_barrier_semaphore()

    def partner(step):
        other = lax.rem(me + lax.rem(step * 37, DEVICES), DEVICES)
        return other, (other // NY, lax.rem(other, NY))

    def greet(step, carry):
        _, where = partner(step)
        pl.semaphore_signal(barrier, inc=1, device_id=where, device_id_type=MESH)
        return carry

    lax.fori_loop(1, DEVICES, greet, 0)
    own = pltpu.make_async_copy(slabs_ref.at[me], recv_ref.at[me], recv_sems.at[mx])
    own.start()
    pl.semaphore_wait(barrier, DEVICES - 1)

    def send(step, carry):
        other, where = partner(step)
        pltpu.make_async_remote_copy(
            src_ref=slabs_ref.at[other],
            dst_ref=recv_ref.at[me],
            send_sem=send_sem,
            recv_sem=recv_sems.at[mx],
            device_id=where,
            device_id_type=MESH,
        ).start()
        return carry

    lax.fori_loop(1, DEVICES, send, 0)

    for group in range(NX):
        here = pl.ds(NY * group, NY)
        pltpu.make_async_copy(slabs_ref.at[here], recv_ref.at[here], recv_sems.at[group]).wait()
        block = recv_ref[here].reshape(NY * SEND_ROWS, 128)
        turned = lax.dot_general(
            block, yf_ref[...], (((0,), (0,)), ((), ())), preferred_element_type=jnp.float32
        )
        for part in range(4):
            half_ref[part, 125 * group : 125 * group + 125, :] = turned[:125, 128 * part : 128 * part + 128]

    def one_pair(pair, carry):
        total = [None, None]
        for chan in range(2):
            source = pair_ref[chan, pair]
            step_x = shift_ref[chan, 2 * pair]
            step_y = shift_ref[chan, 2 * pair + 1]
            rows = pl.ds(source, LAT, stride=25)
            operand = jnp.concatenate(
                [half_ref[2 * chan + half, rows, :] for half in range(2)], axis=1
            ).astype(jnp.bfloat16)
            real = jnp.dot(
                cas_ref[step_x + REACH], operand, preferred_element_type=jnp.float32
            )
            weight = envelope_ref[chan]
            for half in range(2):
                piece = pltpu.roll(real[:, 128 * half : 128 * half + 128], 128 - REACH - step_y, 1)
                term = piece * weight
                total[half] = term if chan == 0 else total[half] + term
        projected = jnp.concatenate(total, axis=1).astype(jnp.bfloat16)
        back = jnp.dot(xb_ref[...], projected, preferred_element_type=jnp.float32)
        for half in range(2):
            back_ref[half, pl.ds(pair, 128, stride=25), :] = back[:, 128 * half : 128 * half + 128]
        return carry

    lax.fori_loop(0, 25, one_pair, 0, unroll=UNROLL)

    def one_group(step, carry):
        group = lax.rem(mx + step, NX)
        rows = pl.ds(pl.multiple_of(200 * group, 8), 128)
        operand = jnp.concatenate(
            [back_ref[half, rows, :] for half in range(2)], axis=1
        ).astype(jnp.bfloat16)
        result = lax.dot_general(
            yb_ref[...], operand, (((1,), (1,)), ((), ())), preferred_element_type=jnp.float32
        ).astype(jnp.bfloat16)
        for lane in range(NY):
            outgoing_ref[NY * group + lane] = result[BACK_ROWS * lane : BACK_ROWS * lane + BACK_ROWS]

        def push(turn, inner):
            lane = lax.rem(my + turn, NY)
            other = NY * group + lane

            @pl.when(other != me)
            def _():
                pltpu.make_async_remote_copy(
                    src_ref=outgoing_ref.at[other],
                    dst_ref=out_ref.at[me],
                    send_sem=back_send_sem,
                    recv_sem=back_sems,
                    device_id=(group, lane),
                    device_id_type=MESH,
                ).start()

            @pl.when(other == me)
            def _():
                pltpu.make_async_copy(outgoing_ref.at[me], out_ref.at[me], back_sems).start()

            return inner

        lax.fori_loop(0, NY, push, 0)
        return carry

    lax.fori_loop(0, NX, one_group, 0)

    most = pl.ds(0, DEVICES - 1)
    pltpu.make_async_copy(slabs_ref.at[most], recv_ref.at[most], send_sem).wait()
    pltpu.make_async_copy(outgoing_ref.at[most], out_ref.at[most], back_send_sem).wait()
    pltpu.make_async_copy(outgoing_ref, out_ref, back_sems).wait()


def transform(slabs, pair_map, bond_shift, envelope):
    smem = pl.BlockSpec(memory_space=pltpu.SMEM)
    vmem = pl.BlockSpec(memory_space=pltpu.VMEM)
    return pl.pallas_call(
        main_kernel,
        out_shape=jax.ShapeDtypeStruct((DEVICES, BACK_ROWS, 128), jnp.bfloat16),
        in_specs=[smem, smem] + [vmem] * 6,
        out_specs=vmem,
        scratch_shapes=[
            pltpu.VMEM((DEVICES, SEND_ROWS, 128), jnp.bfloat16),
            pltpu.VMEM((4, 25 * LAT, 128), jnp.float32),
            pltpu.VMEM((2, 25 * NX * 8, 128), jnp.float32),
            pltpu.VMEM((DEVICES, BACK_ROWS, 128), jnp.bfloat16),
            pltpu.SemaphoreType.DMA,
            pltpu.SemaphoreType.DMA((NX,)),
            pltpu.SemaphoreType.DMA,
            pltpu.SemaphoreType.DMA,
        ],
        compiler_params=pltpu.CompilerParams(
            collective_id=0, has_side_effects=True, vmem_limit_bytes=40 * 2**20
        ),
    )(
        pair_map, bond_shift.reshape(2, 50), slabs,
        jnp.pad(envelope, ((0, 0), (0, 0), (0, 128 - LAT))),
        jnp.asarray(rolled_rows()), jnp.asarray(y_forward()), jnp.asarray(x_back()), jnp.asarray(y_back()),
    )


def local(crossed, vertex, bubble, pair_map, bond_shift, envelope):
    f32 = jnp.float32
    bf16 = jnp.bfloat16
    slabs = crossed.reshape(2, 5, 10, 16, 5, 8, 2, 5).transpose(3, 5, 6, 2, 0, 1, 4, 7)
    slabs = jnp.pad(slabs.reshape(DEVICES, 40, 125), ((0, 0), (0, 0), (0, 3)))
    got = transform(slabs, pair_map, bond_shift, envelope)
    got = got.reshape(DEVICES, 2, 12, 128)[:, :, :10, :125].reshape(16, 8, 2, 10, 5, 5, 5)
    projected = got.transpose(4, 3, 0, 5, 1, 2, 6).reshape(5, 10, ORDER, ORDER)
    vertex = vertex.reshape(5, 10, ORDER, ORDER)

    def apply_bubble(matrix):
        blocked = matrix.reshape(5, 10, NFREQ, NFF, ORDER)
        product = jnp.einsum("xynab,xynbk->xynak", bubble, blocked, preferred_element_type=f32)
        return product.reshape(matrix.shape).astype(bf16)

    out = jnp.einsum("xyij,xyjk->xyik", projected, apply_bubble(vertex), preferred_element_type=f32)
    out = out + jnp.einsum("xyij,xyjk->xyik", vertex, apply_bubble(projected), preferred_element_type=f32)
    return out.astype(bf16).reshape(5, 10, ORDER * ORDER)


def solution(mesh):
    placed = (
        P(None, "kx", "ky", None),
        P("kx", "ky", None),
        P("kx", "ky", None, None, None),
        P(),
        P(),
        P(),
    )
    return jax.shard_map(
        local, mesh=mesh, in_specs=placed, out_specs=P("kx", "ky", None), check_vma=False
    )
```

```python
import math

import jax
import jax.numpy as jnp
import ml_dtypes
import numpy as np
from jax import lax
from jax.experimental import pallas as pl
from jax.experimental.pallas import tpu as pltpu
from jax.sharding import PartitionSpec as P

LAT = 80
NFF = 5
NFREQ = 16
ORDER = 80
NX = 16
NY = 8
DEVICES = NX * NY
QX = LAT // NX
QY = LAT // NY
REACH = 2
SEND_ROWS = 40
BACK_ROWS = 24
UNROLL = 5
BF16 = ml_dtypes.bfloat16
MESH = pl.DeviceIdType.MESH


def cas_table(count):
    phases = np.outer(np.arange(count), np.arange(count)) % count
    angles = phases * (2.0 * math.pi / count)
    return ((np.cos(angles) + np.sin(angles)) / math.sqrt(count)).astype(np.float32)


CAS = cas_table(LAT)


def rolled_rows():
    rows = (np.arange(LAT)[None, :] + np.arange(-REACH, REACH + 1)[:, None]) % LAT
    return CAS[rows].astype(BF16)


def y_forward():
    reach = np.zeros((LAT, 128), np.float32)
    columns = np.arange(LAT + 2 * REACH)
    reach[:, columns] = CAS[:, (columns - REACH) % LAT]
    reach = reach.reshape(NY, QY, 128)
    table = np.zeros((NY, 2, QY, 2, 2, 2, 128), np.float32)
    for chan in range(2):
        for half in range(2):
            table[:, half, :, chan, chan, half] = reach
    return table.reshape(NY * SEND_ROWS, 4 * 128).astype(BF16)


def x_back():
    table = np.zeros((NX, 8, LAT), np.float32)
    table[:, :QX] = CAS.reshape(NX, QX, LAT)
    return table.reshape(NX * 8, LAT).astype(BF16)


def y_back():
    table = np.zeros((NY, 2, 12, 2, 128), np.float32)
    for half in range(2):
        table[:, half, :QY, half, :LAT] = CAS.reshape(NY, QY, LAT)
    return table.reshape(NY * BACK_ROWS, 2 * 128).astype(BF16)


def spread_source():
    table = np.zeros((112 + 400 + 112, 16 * 32), np.float32)
    a, n2, b = np.meshgrid(np.arange(5), np.arange(16), np.arange(5), indexing="ij")
    table[112 + 80 * a + 5 * n2 + b, 32 * n2 + 5 * a + b] = 1
    return table.astype(BF16)


def merge_x():
    table = np.zeros((5, 4, 32, 4, 128), np.float32)
    qx, g, pair = np.meshgrid(np.arange(5), np.arange(4), np.arange(25), indexing="ij")
    table[qx, g, pair, g, 25 * qx + pair] = 1
    return table.reshape(640, 512).astype(BF16)


def split_x():
    return np.ascontiguousarray(merge_x().T)


def gather_rows():
    table = np.zeros((16, 32, 5, 128), np.float32)
    a, n2, b = np.meshgrid(np.arange(5), np.arange(16), np.arange(5), indexing="ij")
    table[n2, 5 * a + b, a, 5 * n2 + b] = 1
    return table.reshape(512, 640).astype(BF16)


def turn_columns():
    table = np.zeros((80, 128), np.float32)
    n, a = np.meshgrid(np.arange(16), np.arange(5), indexing="ij")
    table[5 * n + a, 16 * a + n] = 1
    return table.astype(BF16)


def same_frequency():
    table = np.zeros((16, 128), np.float32)
    n, b = np.meshgrid(np.arange(16), np.arange(5), indexing="ij")
    table[n, 16 * b + n] = 1
    return table


def f32dot(left, right, dims=((1,), (0,))):
    return lax.dot_general(left, right, (dims, ((), ())), preferred_element_type=jnp.float32)


def build_slabs(crossed_ref, spread_ref, merge_ref, mixed_ref, slabs_ref):
    for n in range(NFREQ):
        start = 400 * n // 128 * 128
        offset = 400 * n - start
        spread = f32dot(crossed_ref[:, start : start + 512], spread_ref[112 - offset : 624 - offset, :])
        for part in range(4):
            for qx in range(QX):
                mixed_ref[part, qx, 20 * n : 20 * n + 20, :] = spread[
                    20 * qx : 20 * qx + 20, 128 * part : 128 * part + 128
                ]

    def one_part(part, carry):
        rows = jnp.concatenate([mixed_ref[part, qx] for qx in range(QX)], axis=1).astype(jnp.bfloat16)
        merged = f32dot(rows, merge_ref[...]).astype(jnp.bfloat16)
        for g in range(4):
            for pair in range(8):
                slabs_ref[(4 * part + g) * 8 + pair] = merged[
                    40 * pair : 40 * pair + 40, 128 * g : 128 * g + 128
                ]
        return carry

    lax.fori_loop(0, 4, one_part, 0)


def prepare_vertex(vertex_ref, bubble_ref, turn_ref, same_ref, rows_ref, left_ref, right_ref):
    for qx in range(QX):
        for i in range(ORDER):
            rows_ref[80 * i + 16 * qx : 80 * i + 16 * qx + 10, :80] = vertex_ref[
                qx, :, 80 * i : 80 * i + 80
            ].astype(jnp.float32)
    same = same_ref[...]

    def one(q, carry):
        at = q + 6 * (q // 10)
        block = jnp.concatenate(
            [rows_ref[pl.ds(80 * a + at, 16, stride=400), :] for a in range(5)], axis=0
        ).astype(jnp.bfloat16)
        bubble = jnp.concatenate(
            [bubble_ref[pl.ds(5 * q + a, 1), :] * same for a in range(5)], axis=0
        ).astype(jnp.bfloat16)
        turned = f32dot(block[:, :80], turn_ref[...]).astype(jnp.bfloat16)
        right_ref[q] = f32dot(turned[:, :80], bubble).astype(jnp.bfloat16)
        left = f32dot(bubble[:, :80], block)
        for a in range(5):
            left_ref[pl.ds(80 * q + a, 16, stride=5), :] = left[16 * a : 16 * a + 16]
        return carry

    lax.fori_loop(0, QX * QY, one, 0, unroll=5)


def finish(got_ref, split_ref, gather_ref, spread_ref, blocks_ref, left_ref, right_ref, rows_ref, out_ref):
    for part in range(4):
        rows = jnp.concatenate(
            [got_ref[8 * (4 * part + g) : 8 * (4 * part + g) + 8].reshape(192, 128) for g in range(4)], axis=1
        )
        apart = f32dot(rows, split_ref[...]).astype(jnp.bfloat16)
        for qx in range(QX):
            spread_ref[qx, :, 128 * part : 128 * part + 128] = apart[:, 128 * qx : 128 * qx + 128]
    for qx in range(QX):
        found = f32dot(spread_ref[qx], gather_ref[...])
        for a in range(5):
            blocks_ref[a, 192 * qx : 192 * qx + 192, :] = found[:, 128 * a : 128 * a + 128]

    def one(q, carry):
        at = q + 182 * (q // 10)
        block = jnp.concatenate(
            [blocks_ref[a, pl.ds(at, 16, stride=12), :] for a in range(5)], axis=0
        ).astype(jnp.bfloat16)
        left = left_ref[pl.ds(pl.multiple_of(80 * q, 8), 80), :].astype(jnp.bfloat16)
        result = f32dot(block[:, :80], left) + f32dot(right_ref[q][:, :80], block)
        put = q + 6 * (q // 10)
        for a in range(5):
            rows_ref[pl.ds(80 * a + put, 16, stride=400), :] = result[16 * a : 16 * a + 16]
        return carry

    lax.fori_loop(0, QX * QY, one, 0, unroll=5)
    for qx in range(QX):
        for i in range(0, ORDER, 8):
            wide = jnp.concatenate(
                [rows_ref[80 * (i + k) + 16 * qx : 80 * (i + k) + 16 * qx + 16, :80] for k in range(8)], axis=1
            ).astype(jnp.bfloat16)
            out_ref[qx, :, 80 * i : 80 * i + 640] = wide[:10]


def main_kernel(
    pair_ref, shift_ref, crossed_ref, vertex_ref, bubble_ref, envelope_ref,
    cas_ref, yf_ref, xb_ref, yb_ref, spread_ref, merge_ref, split_ref, gather_ref, turn_ref, same_ref,
    out_ref,
    mixed_ref, slabs_ref, recv_ref, half_ref, back_ref, outgoing_ref, got_ref,
    vertex_rows_ref, left_ref, right_ref, spread_back_ref, blocks_ref, out_rows_ref,
    send_sem, recv_sems, back_send_sem, back_sem,
):
    mx = lax.axis_index("kx")
    my = lax.axis_index("ky")
    me = mx * NY + my
    barrier = pltpu.get_barrier_semaphore()

    def partner(step):
        other = lax.rem(me + lax.rem(step * 37, DEVICES), DEVICES)
        return other, (other // NY, lax.rem(other, NY))

    def greet(step, carry):
        _, where = partner(step)
        pl.semaphore_signal(barrier, inc=1, device_id=where, device_id_type=MESH)
        return carry

    lax.fori_loop(1, DEVICES, greet, 0)
    build_slabs(crossed_ref, spread_ref, merge_ref, mixed_ref, slabs_ref)
    own = pltpu.make_async_copy(slabs_ref.at[me], recv_ref.at[me], recv_sems.at[mx])
    own.start()
    pl.semaphore_wait(barrier, DEVICES - 1)

    def send(step, carry):
        other, where = partner(step)
        pltpu.make_async_remote_copy(
            src_ref=slabs_ref.at[other],
            dst_ref=recv_ref.at[me],
            send_sem=send_sem,
            recv_sem=recv_sems.at[mx],
            device_id=where,
            device_id_type=MESH,
        ).start()
        return carry

    lax.fori_loop(1, DEVICES, send, 0)
    prepare_vertex(vertex_ref, bubble_ref, turn_ref, same_ref, vertex_rows_ref, left_ref, right_ref)

    for group in range(NX):
        here = pl.ds(NY * group, NY)
        pltpu.make_async_copy(slabs_ref.at[here], recv_ref.at[here], recv_sems.at[group]).wait()
        block = recv_ref[here].reshape(NY * SEND_ROWS, 128)
        turned = f32dot(block, yf_ref[...], ((0,), (0,)))
        for part in range(4):
            half_ref[part, 125 * group : 125 * group + 125, :] = turned[:125, 128 * part : 128 * part + 128]

    def one_pair(pair, carry):
        total = [None, None]
        for chan in range(2):
            source = pair_ref[chan, pair]
            step_x = shift_ref[chan, 2 * pair]
            step_y = shift_ref[chan, 2 * pair + 1]
            rows = pl.ds(source, LAT, stride=25)
            operand = jnp.concatenate(
                [half_ref[2 * chan + half, rows, :] for half in range(2)], axis=1
            ).astype(jnp.bfloat16)
            real = f32dot(cas_ref[step_x + REACH], operand)
            weight = envelope_ref[chan]
            for half in range(2):
                piece = pltpu.roll(real[:, 128 * half : 128 * half + 128], 128 - REACH - step_y, 1)
                term = piece * weight
                total[half] = term if chan == 0 else total[half] + term
        projected = jnp.concatenate(total, axis=1).astype(jnp.bfloat16)
        back = f32dot(xb_ref[...], projected)
        for half in range(2):
            back_ref[half, pl.ds(pair, 128, stride=25), :] = back[:, 128 * half : 128 * half + 128]
        return carry

    lax.fori_loop(0, 25, one_pair, 0, unroll=UNROLL)

    def one_group(step, carry):
        group = lax.rem(mx + step, NX)
        rows = pl.ds(pl.multiple_of(200 * group, 8), 128)
        operand = jnp.concatenate(
            [back_ref[half, rows, :] for half in range(2)], axis=1
        ).astype(jnp.bfloat16)
        result = f32dot(yb_ref[...], operand, ((1,), (1,))).astype(jnp.bfloat16)
        for lane in range(NY):
            outgoing_ref[NY * group + lane] = result[BACK_ROWS * lane : BACK_ROWS * lane + BACK_ROWS]

        def push(turn, inner):
            lane = lax.rem(my + turn, NY)
            other = NY * group + lane

            @pl.when(other != me)
            def _():
                pltpu.make_async_remote_copy(
                    src_ref=outgoing_ref.at[other],
                    dst_ref=got_ref.at[me],
                    send_sem=back_send_sem,
                    recv_sem=back_sem,
                    device_id=(group, lane),
                    device_id_type=MESH,
                ).start()

            @pl.when(other == me)
            def _():
                pltpu.make_async_copy(outgoing_ref.at[me], got_ref.at[me], back_sem).start()

            return inner

        lax.fori_loop(0, NY, push, 0)
        return carry

    lax.fori_loop(0, NX, one_group, 0)

    most = pl.ds(0, DEVICES - 1)
    pltpu.make_async_copy(slabs_ref.at[most], recv_ref.at[most], send_sem).wait()
    pltpu.make_async_copy(outgoing_ref, got_ref, back_sem).wait()
    finish(
        got_ref, split_ref, gather_ref, spread_back_ref, blocks_ref, left_ref, right_ref, out_rows_ref, out_ref
    )
    pltpu.make_async_copy(outgoing_ref.at[most], got_ref.at[most], back_send_sem).wait()


def local(crossed, vertex, bubble, pair_map, bond_shift, envelope):
    f32 = jnp.float32
    bf16 = jnp.bfloat16
    crossed = crossed.transpose(1, 2, 0, 3).reshape(QX * QY * 2, ORDER * ORDER)
    bubble = bubble.transpose(0, 1, 3, 4, 2).reshape(250, 80).astype(f32)
    bubble = jnp.pad(bubble, ((0, 0), (0, 48)))
    envelope = jnp.pad(envelope, ((0, 0), (0, 0), (0, 128 - LAT)))
    tables = [
        rolled_rows(), y_forward(), x_back(), y_back(), spread_source(), merge_x(), split_x(), gather_rows(),
        turn_columns(), same_frequency(),
    ]
    smem = pl.BlockSpec(memory_space=pltpu.SMEM)
    vmem = pl.BlockSpec(memory_space=pltpu.VMEM)
    return pl.pallas_call(
        main_kernel,
        out_shape=jax.ShapeDtypeStruct(vertex.shape, bf16),
        in_specs=[smem, smem] + [vmem] * (4 + len(tables)),
        out_specs=vmem,
        scratch_shapes=[
            pltpu.VMEM((4, QX, 20 * NFREQ, 128), f32),
            pltpu.VMEM((DEVICES, SEND_ROWS, 128), bf16),
            pltpu.VMEM((DEVICES, SEND_ROWS, 128), bf16),
            pltpu.VMEM((4, 25 * LAT, 128), f32),
            pltpu.VMEM((2, 25 * NX * 8, 128), f32),
            pltpu.VMEM((DEVICES, BACK_ROWS, 128), bf16),
            pltpu.VMEM((DEVICES, BACK_ROWS, 128), bf16),
            pltpu.VMEM((80 * ORDER, 128), f32),
            pltpu.VMEM((QX * QY * ORDER, 128), f32),
            pltpu.VMEM((QX * QY, ORDER, 128), bf16),
            pltpu.VMEM((QX, 192, 512), bf16),
            pltpu.VMEM((5, 192 * QX, 128), f32),
            pltpu.VMEM((80 * ORDER, 128), f32),
            pltpu.SemaphoreType.DMA,
            pltpu.SemaphoreType.DMA((NX,)),
            pltpu.SemaphoreType.DMA,
            pltpu.SemaphoreType.DMA,
        ],
        compiler_params=pltpu.CompilerParams(
            collective_id=0, has_side_effects=True, vmem_limit_bytes=56 * 2**20
        ),
    )(
        pair_map, bond_shift.reshape(2, 50), crossed, vertex, bubble, envelope,
        *[jnp.asarray(table) for table in tables],
    )


def solution(mesh):
    placed = (
        P(None, "kx", "ky", None),
        P("kx", "ky", None),
        P("kx", "ky", None, None, None),
        P(),
        P(),
        P(),
    )
    return jax.shard_map(
        local, mesh=mesh, in_specs=placed, out_specs=P("kx", "ky", None), check_vma=False
    )
```

```python
import math

import jax
import jax.numpy as jnp
import ml_dtypes
import numpy as np
from jax import lax
from jax.experimental import pallas as pl
from jax.experimental.pallas import tpu as pltpu
from jax.sharding import PartitionSpec as P

LAT = 80
NFF = 5
NFREQ = 16
ORDER = 80
NX = 16
NY = 8
DEVICES = NX * NY
QX = LAT // NX
QY = LAT // NY
REACH = 2
SEND_ROWS = 40
BACK_ROWS = 24
UNROLL = 5
BF16 = ml_dtypes.bfloat16
MESH = pl.DeviceIdType.MESH


def cas_table(count):
    phases = np.outer(np.arange(count), np.arange(count)) % count
    angles = phases * (2.0 * math.pi / count)
    return ((np.cos(angles) + np.sin(angles)) / math.sqrt(count)).astype(np.float32)


CAS = cas_table(LAT)


def rolled_rows():
    rows = (np.arange(LAT)[None, :] + np.arange(-REACH, REACH + 1)[:, None]) % LAT
    return CAS[rows].astype(BF16)


def y_forward():
    reach = np.zeros((LAT, 128), np.float32)
    columns = np.arange(LAT + 2 * REACH)
    reach[:, columns] = CAS[:, (columns - REACH) % LAT]
    reach = reach.reshape(NY, QY, 128)
    table = np.zeros((NY, 2, QY, 2, 2, 2, 128), np.float32)
    for chan in range(2):
        for half in range(2):
            table[:, half, :, chan, chan, half] = reach
    return table.reshape(NY * SEND_ROWS, 4 * 128).astype(BF16)


def x_back():
    table = np.zeros((NX, 8, LAT), np.float32)
    table[:, :QX] = CAS.reshape(NX, QX, LAT)
    return table.reshape(NX * 8, LAT).astype(BF16)


def y_back():
    table = np.zeros((NY, 2, 12, 2, 128), np.float32)
    for half in range(2):
        table[:, half, :QY, half, :LAT] = CAS.reshape(NY, QY, LAT)
    return table.reshape(NY * BACK_ROWS, 2 * 128).astype(BF16)


def spread_source():
    table = np.zeros((112 + 400 + 112, 16 * 32), np.float32)
    a, n2, b = np.meshgrid(np.arange(5), np.arange(16), np.arange(5), indexing="ij")
    table[112 + 80 * a + 5 * n2 + b, 32 * n2 + 5 * a + b] = 1
    return table.astype(BF16)


def merge_x():
    table = np.zeros((5, 4, 32, 4, 128), np.float32)
    qx, g, pair = np.meshgrid(np.arange(5), np.arange(4), np.arange(25), indexing="ij")
    table[qx, g, pair, g, 25 * qx + pair] = 1
    return table.reshape(640, 512).astype(BF16)


def split_x():
    return np.ascontiguousarray(merge_x().T)


def gather_rows():
    table = np.zeros((16, 32, 5, 128), np.float32)
    a, n2, b = np.meshgrid(np.arange(5), np.arange(16), np.arange(5), indexing="ij")
    table[n2, 5 * a + b, a, 5 * n2 + b] = 1
    return table.reshape(512, 640).astype(BF16)


def turn_columns():
    table = np.zeros((80, 128), np.float32)
    n, a = np.meshgrid(np.arange(16), np.arange(5), indexing="ij")
    table[5 * n + a, 16 * a + n] = 1
    return table.astype(BF16)


def same_frequency():
    table = np.zeros((16, 128), np.float32)
    n, b = np.meshgrid(np.arange(16), np.arange(5), indexing="ij")
    table[n, 16 * b + n] = 1
    return table


def f32dot(left, right, dims=((1,), (0,))):
    return lax.dot_general(left, right, (dims, ((), ())), preferred_element_type=jnp.float32)


def build_slabs(crossed_ref, spread_ref, merge_ref, mixed_ref, slabs_ref):
    for n in range(NFREQ):
        start = 400 * n // 128 * 128
        offset = 400 * n - start
        rows = crossed_ref[:, :, start : start + 512].reshape(2 * QX * QY, 512)
        spread = f32dot(rows, spread_ref[112 - offset : 624 - offset, :])
        for part in range(4):
            for qx in range(QX):
                mixed_ref[part, qx, 20 * n : 20 * n + 20, :] = spread[
                    20 * qx : 20 * qx + 20, 128 * part : 128 * part + 128
                ]

    def one_part(part, carry):
        rows = jnp.concatenate([mixed_ref[part, qx] for qx in range(QX)], axis=1).astype(jnp.bfloat16)
        merged = f32dot(rows, merge_ref[...]).astype(jnp.bfloat16)
        for g in range(4):
            for pair in range(8):
                slabs_ref[(4 * part + g) * 8 + pair] = merged[
                    40 * pair : 40 * pair + 40, 128 * g : 128 * g + 128
                ]
        return carry

    lax.fori_loop(0, 4, one_part, 0)


def prepare_vertex(
    vertex_ref, bubble_ref, turn_ref, same_ref, rows_ref, wide_ref, lines_ref, left_ref, right_ref
):
    for qx in range(QX):
        for i in range(ORDER):
            rows_ref[80 * i + 16 * qx : 80 * i + 16 * qx + 10, :80] = vertex_ref[
                qx, :, 80 * i : 80 * i + 80
            ].astype(jnp.float32)
    same = same_ref[...]
    wide_ref[:, :5, :16] = bubble_ref[...].reshape(250, 5, 16).astype(jnp.float32)
    lines_ref[:, :80] = jnp.concatenate([wide_ref[:, b, :16] for b in range(5)], axis=1)

    def one(q, carry):
        at = q + 6 * (q // 10)
        block = jnp.concatenate(
            [rows_ref[pl.ds(80 * a + at, 16, stride=400), :] for a in range(5)], axis=0
        ).astype(jnp.bfloat16)
        bubble = jnp.concatenate(
            [lines_ref[pl.ds(5 * q + a, 1), :] * same for a in range(5)], axis=0
        ).astype(jnp.bfloat16)
        turned = f32dot(block[:, :80], turn_ref[...]).astype(jnp.bfloat16)
        right_ref[q] = f32dot(turned[:, :80], bubble).astype(jnp.bfloat16)
        left = f32dot(bubble[:, :80], block)
        for a in range(5):
            left_ref[pl.ds(80 * q + a, 16, stride=5), :] = left[16 * a : 16 * a + 16]
        return carry

    lax.fori_loop(0, QX * QY, one, 0, unroll=5)


def finish(got_ref, split_ref, gather_ref, spread_ref, blocks_ref, left_ref, right_ref, rows_ref, out_ref):
    for part in range(4):
        rows = jnp.concatenate(
            [got_ref[8 * (4 * part + g) : 8 * (4 * part + g) + 8].reshape(192, 128) for g in range(4)], axis=1
        )
        apart = f32dot(rows, split_ref[...]).astype(jnp.bfloat16)
        for qx in range(QX):
            spread_ref[qx, :, 128 * part : 128 * part + 128] = apart[:, 128 * qx : 128 * qx + 128]
    for qx in range(QX):
        found = f32dot(spread_ref[qx], gather_ref[...])
        for a in range(5):
            blocks_ref[a, 192 * qx : 192 * qx + 192, :] = found[:, 128 * a : 128 * a + 128]

    def one(q, carry):
        at = q + 182 * (q // 10)
        block = jnp.concatenate(
            [blocks_ref[a, pl.ds(at, 16, stride=12), :] for a in range(5)], axis=0
        ).astype(jnp.bfloat16)
        left = left_ref[pl.ds(pl.multiple_of(80 * q, 8), 80), :].astype(jnp.bfloat16)
        result = f32dot(block[:, :80], left) + f32dot(right_ref[q][:, :80], block)
        put = q + 6 * (q // 10)
        for a in range(5):
            rows_ref[pl.ds(80 * a + put, 16, stride=400), :] = result[16 * a : 16 * a + 16]
        return carry

    lax.fori_loop(0, QX * QY, one, 0, unroll=5)
    for qx in range(QX):
        for i in range(0, ORDER, 8):
            wide = jnp.concatenate(
                [rows_ref[80 * (i + k) + 16 * qx : 80 * (i + k) + 16 * qx + 16, :80] for k in range(8)], axis=1
            ).astype(jnp.bfloat16)
            out_ref[qx, :, 80 * i : 80 * i + 640] = wide[:10]


def main_kernel(
    pair_ref, shift_ref, envelope_ref, xb_ref, yb_ref, turn_ref, same_ref,
    crossed_hbm, spread_hbm, merge_hbm, vertex_hbm, bubble_hbm, yf_hbm, cas_hbm, split_hbm, gather_hbm,
    out_ref,
    crossed_ref, spread_ref, merge_ref, vertex_ref, bubble_ref, yf_ref, cas_ref, split_ref, gather_ref,
    mixed_ref, slabs_ref, recv_ref, half_ref, back_ref, outgoing_ref, got_ref, weight_ref,
    vertex_rows_ref, wide_ref, lines_ref, left_ref, right_ref, spread_back_ref, blocks_ref, out_rows_ref,
    load_sems, send_sem, recv_sems, back_send_sem, back_sem,
):
    sources = (crossed_hbm, spread_hbm, merge_hbm, vertex_hbm, bubble_hbm, yf_hbm, cas_hbm, split_hbm, gather_hbm)
    places = (crossed_ref, spread_ref, merge_ref, vertex_ref, bubble_ref, yf_ref, cas_ref, split_ref, gather_ref)
    loads = [
        pltpu.make_async_copy(source, place, load_sems.at[k])
        for k, (source, place) in enumerate(zip(sources, places))
    ]
    for load in loads:
        load.start()
    mx = lax.axis_index("kx")
    my = lax.axis_index("ky")
    me = mx * NY + my
    barrier = pltpu.get_barrier_semaphore()

    def partner(step):
        other = lax.rem(me + lax.rem(step * 37, DEVICES), DEVICES)
        return other, (other // NY, lax.rem(other, NY))

    def greet(step, carry):
        _, where = partner(step)
        pl.semaphore_signal(barrier, inc=1, device_id=where, device_id_type=MESH)
        return carry

    lax.fori_loop(1, DEVICES, greet, 0)
    for load in loads[:3]:
        load.wait()
    build_slabs(crossed_ref, spread_ref, merge_ref, mixed_ref, slabs_ref)
    own = pltpu.make_async_copy(slabs_ref.at[me], recv_ref.at[me], recv_sems.at[mx])
    own.start()
    pl.semaphore_wait(barrier, DEVICES - 1)

    def send(step, carry):
        other, where = partner(step)
        pltpu.make_async_remote_copy(
            src_ref=slabs_ref.at[other],
            dst_ref=recv_ref.at[me],
            send_sem=send_sem,
            recv_sem=recv_sems.at[mx],
            device_id=where,
            device_id_type=MESH,
        ).start()
        return carry

    lax.fori_loop(1, DEVICES, send, 0)
    weight_ref[...] = jnp.zeros_like(weight_ref)
    weight_ref[:, :, :LAT] = envelope_ref[...]
    for load in loads[3:]:
        load.wait()
    prepare_vertex(
        vertex_ref, bubble_ref, turn_ref, same_ref, vertex_rows_ref, wide_ref, lines_ref, left_ref, right_ref
    )

    for group in range(NX):
        here = pl.ds(NY * group, NY)
        pltpu.make_async_copy(slabs_ref.at[here], recv_ref.at[here], recv_sems.at[group]).wait()
        block = recv_ref[here].reshape(NY * SEND_ROWS, 128)
        turned = f32dot(block, yf_ref[...], ((0,), (0,)))
        for part in range(4):
            half_ref[part, 125 * group : 125 * group + 125, :] = turned[:125, 128 * part : 128 * part + 128]

    def one_pair(pair, carry):
        total = [None, None]
        for chan in range(2):
            source = pair_ref[chan, pair]
            step_x = shift_ref[chan, pair // 5, 0, lax.rem(pair, 5)]
            step_y = shift_ref[chan, pair // 5, 1, lax.rem(pair, 5)]
            rows = pl.ds(source, LAT, stride=25)
            operand = jnp.concatenate(
                [half_ref[2 * chan + half, rows, :] for half in range(2)], axis=1
            ).astype(jnp.bfloat16)
            real = f32dot(cas_ref[step_x + REACH], operand)
            weight = weight_ref[chan]
            for half in range(2):
                piece = pltpu.roll(real[:, 128 * half : 128 * half + 128], 128 - REACH - step_y, 1)
                term = piece * weight
                total[half] = term if chan == 0 else total[half] + term
        projected = jnp.concatenate(total, axis=1).astype(jnp.bfloat16)
        back = f32dot(xb_ref[...], projected)
        for half in range(2):
            back_ref[half, pl.ds(pair, 128, stride=25), :] = back[:, 128 * half : 128 * half + 128]
        return carry

    lax.fori_loop(0, 25, one_pair, 0, unroll=UNROLL)

    def one_group(step, carry):
        group = lax.rem(mx + step, NX)
        rows = pl.ds(pl.multiple_of(200 * group, 8), 128)
        operand = jnp.concatenate(
            [back_ref[half, rows, :] for half in range(2)], axis=1
        ).astype(jnp.bfloat16)
        result = f32dot(yb_ref[...], operand, ((1,), (1,))).astype(jnp.bfloat16)
        for lane in range(NY):
            outgoing_ref[NY * group + lane] = result[BACK_ROWS * lane : BACK_ROWS * lane + BACK_ROWS]

        def push(turn, inner):
            lane = lax.rem(my + turn, NY)
            other = NY * group + lane

            @pl.when(other != me)
            def _():
                pltpu.make_async_remote_copy(
                    src_ref=outgoing_ref.at[other],
                    dst_ref=got_ref.at[me],
                    send_sem=back_send_sem,
                    recv_sem=back_sem,
                    device_id=(group, lane),
                    device_id_type=MESH,
                ).start()

            @pl.when(other == me)
            def _():
                pltpu.make_async_copy(outgoing_ref.at[me], got_ref.at[me], back_sem).start()

            return inner

        lax.fori_loop(0, NY, push, 0)
        return carry

    lax.fori_loop(0, NX, one_group, 0)

    most = pl.ds(0, DEVICES - 1)
    pltpu.make_async_copy(slabs_ref.at[most], recv_ref.at[most], send_sem).wait()
    pltpu.make_async_copy(outgoing_ref, got_ref, back_sem).wait()
    finish(
        got_ref, split_ref, gather_ref, spread_back_ref, blocks_ref, left_ref, right_ref, out_rows_ref, out_ref
    )
    pltpu.make_async_copy(outgoing_ref.at[most], got_ref.at[most], back_send_sem).wait()


def local(crossed, vertex, bubble, pair_map, bond_shift, envelope):
    f32 = jnp.float32
    bf16 = jnp.bfloat16
    crossed = crossed.transpose(1, 2, 0, 3).reshape(QX * QY, 2, ORDER * ORDER)
    bubble = bubble.transpose(0, 1, 3, 4, 2).reshape(QX * QY, NFF, NFF, NFREQ)
    bond_shift = bond_shift.transpose(0, 1, 3, 2)
    small = [x_back(), y_back(), turn_columns(), same_frequency()]
    small = [jnp.asarray(table) for table in small]
    large = [
        crossed, jnp.asarray(spread_source()), jnp.asarray(merge_x()), vertex, bubble,
        jnp.asarray(y_forward()), jnp.asarray(rolled_rows()), jnp.asarray(split_x()), jnp.asarray(gather_rows()),
    ]
    smem = pl.BlockSpec(memory_space=pltpu.SMEM)
    vmem = pl.BlockSpec(memory_space=pltpu.VMEM)
    hbm = pl.BlockSpec(memory_space=pl.ANY)
    return pl.pallas_call(
        main_kernel,
        out_shape=jax.ShapeDtypeStruct(vertex.shape, bf16),
        in_specs=[smem, smem, vmem] + [vmem] * len(small) + [hbm] * len(large),
        out_specs=vmem,
        scratch_shapes=[pltpu.VMEM(array.shape, array.dtype) for array in large] + [
            pltpu.VMEM((4, QX, 20 * NFREQ, 128), f32),
            pltpu.VMEM((DEVICES, SEND_ROWS, 128), bf16),
            pltpu.VMEM((DEVICES, SEND_ROWS, 128), bf16),
            pltpu.VMEM((4, 25 * LAT, 128), f32),
            pltpu.VMEM((2, 25 * NX * 8, 128), f32),
            pltpu.VMEM((DEVICES, BACK_ROWS, 128), bf16),
            pltpu.VMEM((DEVICES, BACK_ROWS, 128), bf16),
            pltpu.VMEM((2, LAT, 128), f32),
            pltpu.VMEM((80 * ORDER, 128), f32),
            pltpu.VMEM((250, 8, 128), f32),
            pltpu.VMEM((250, 128), f32),
            pltpu.VMEM((QX * QY * ORDER, 128), f32),
            pltpu.VMEM((QX * QY, ORDER, 128), bf16),
            pltpu.VMEM((QX, 192, 512), bf16),
            pltpu.VMEM((5, 192 * QX, 128), f32),
            pltpu.VMEM((80 * ORDER, 128), f32),
            pltpu.SemaphoreType.DMA((len(large),)),
            pltpu.SemaphoreType.DMA,
            pltpu.SemaphoreType.DMA((NX,)),
            pltpu.SemaphoreType.DMA,
            pltpu.SemaphoreType.DMA,
        ],
        compiler_params=pltpu.CompilerParams(
            collective_id=0, has_side_effects=True, vmem_limit_bytes=60 * 2**20
        ),
    )(pair_map, bond_shift, envelope, *small, *large)


def solution(mesh):
    placed = (
        P(None, "kx", "ky", None),
        P("kx", "ky", None),
        P("kx", "ky", None, None, None),
        P(),
        P(),
        P(),
    )
    return jax.shard_map(
        local, mesh=mesh, in_specs=placed, out_specs=P("kx", "ky", None), check_vma=False
    )
```

```python
import math

import jax
import jax.numpy as jnp
import ml_dtypes
import numpy as np
from jax import lax
from jax.experimental import pallas as pl
from jax.experimental.pallas import tpu as pltpu
from jax.sharding import PartitionSpec as P

LAT = 80
NFF = 5
NFREQ = 16
ORDER = 80
NX = 16
NY = 8
DEVICES = NX * NY
QX = LAT // NX
QY = LAT // NY
REACH = 2
SEND_ROWS = 40
BACK_ROWS = 24
BATCH = 25
BF16 = ml_dtypes.bfloat16
MESH = pl.DeviceIdType.MESH


def cas_table(count):
    phases = np.outer(np.arange(count), np.arange(count)) % count
    angles = phases * (2.0 * math.pi / count)
    return ((np.cos(angles) + np.sin(angles)) / math.sqrt(count)).astype(np.float32)


CAS = cas_table(LAT)


def rolled_rows():
    rows = (np.arange(LAT)[None, :] + np.arange(-REACH, REACH + 1)[:, None]) % LAT
    return CAS[rows].astype(BF16)


def y_forward():
    reach = np.zeros((LAT, 128), np.float32)
    columns = np.arange(LAT + 2 * REACH)
    reach[:, columns] = CAS[:, (columns - REACH) % LAT]
    reach = reach.reshape(NY, QY, 128)
    table = np.zeros((NY, 2, QY, 2, 2, 2, 128), np.float32)
    for chan in range(2):
        for half in range(2):
            table[:, half, :, chan, chan, half] = reach
    return table.reshape(NY * SEND_ROWS, 4 * 128).astype(BF16)


def x_back():
    table = np.zeros((NX, 8, LAT), np.float32)
    table[:, :QX] = CAS.reshape(NX, QX, LAT)
    return table.reshape(NX * 8, LAT).astype(BF16)


def y_back():
    table = np.zeros((NY, 2, 12, 2, 128), np.float32)
    for half in range(2):
        table[:, half, :QY, half, :LAT] = CAS.reshape(NY, QY, LAT)
    return table.reshape(NY * BACK_ROWS, 2 * 128).astype(BF16)


def spread_source():
    table = np.zeros((112 + 400 + 112, 16 * 32), np.float32)
    a, n2, b = np.meshgrid(np.arange(5), np.arange(16), np.arange(5), indexing="ij")
    table[112 + 80 * a + 5 * n2 + b, 32 * n2 + 5 * a + b] = 1
    return table.astype(BF16)


def merge_x():
    table = np.zeros((5, 4, 32, 4, 128), np.float32)
    qx, g, pair = np.meshgrid(np.arange(5), np.arange(4), np.arange(25), indexing="ij")
    table[qx, g, pair, g, 25 * qx + pair] = 1
    return table.reshape(640, 512).astype(BF16)


def split_x():
    return np.ascontiguousarray(merge_x().T)


def gather_rows():
    table = np.zeros((16, 32, 5, 128), np.float32)
    a, n2, b = np.meshgrid(np.arange(5), np.arange(16), np.arange(5), indexing="ij")
    table[n2, 5 * a + b, a, 5 * n2 + b] = 1
    return table.reshape(512, 640).astype(BF16)


def turn_columns():
    table = np.zeros((80, 128), np.float32)
    n, a = np.meshgrid(np.arange(16), np.arange(5), indexing="ij")
    table[5 * n + a, 16 * a + n] = 1
    return table.astype(BF16)


def same_frequency():
    table = np.zeros((16, 128), np.float32)
    n, b = np.meshgrid(np.arange(16), np.arange(5), indexing="ij")
    table[n, 16 * b + n] = 1
    return table


def f32dot(left, right, dims=((1,), (0,))):
    return lax.dot_general(left, right, (dims, ((), ())), preferred_element_type=jnp.float32)


def build_slabs(crossed_ref, spread_ref, merge_ref, mixed_ref, slabs_ref):
    for n in range(NFREQ):
        start = 400 * n // 128 * 128
        offset = 400 * n - start
        rows = crossed_ref[:, :, start : start + 512].reshape(2 * QX * QY, 512)
        spread = f32dot(rows, spread_ref[112 - offset : 624 - offset, :])
        for part in range(4):
            for qx in range(QX):
                mixed_ref[part, qx, 20 * n : 20 * n + 20, :] = spread[
                    20 * qx : 20 * qx + 20, 128 * part : 128 * part + 128
                ]

    def one_part(part, carry):
        rows = jnp.concatenate([mixed_ref[part, qx] for qx in range(QX)], axis=1).astype(jnp.bfloat16)
        merged = f32dot(rows, merge_ref[...]).astype(jnp.bfloat16)
        for g in range(4):
            for pair in range(8):
                slabs_ref[(4 * part + g) * 8 + pair] = merged[
                    40 * pair : 40 * pair + 40, 128 * g : 128 * g + 128
                ]
        return carry

    for part in range(4):
        one_part(part, 0)


def prepare_vertex(
    vertex_ref, bubble_ref, turn_ref, same_ref, rows_ref, wide_ref, lines_ref, left_ref, right_ref
):
    for qx in range(QX):
        for i in range(ORDER):
            rows_ref[80 * i + 16 * qx : 80 * i + 16 * qx + 10, :80] = vertex_ref[
                qx, :, 80 * i : 80 * i + 80
            ].astype(jnp.float32)
    same = same_ref[...]
    wide_ref[:, :5, :16] = bubble_ref[...].reshape(250, 5, 16).astype(jnp.float32)
    lines_ref[:, :80] = jnp.concatenate([wide_ref[:, b, :16] for b in range(5)], axis=1)

    for start in range(0, QX * QY, BATCH):
        batch = range(start, start + BATCH)
        blocks = []
        bubbles = []
        for q in batch:
            at = q + 6 * (q // 10)
            blocks.append(
                jnp.concatenate(
                    [rows_ref[pl.ds(80 * a + at, 16, stride=400), :] for a in range(5)], axis=0
                ).astype(jnp.bfloat16)
            )
            bubbles.append(
                jnp.concatenate(
                    [lines_ref[pl.ds(5 * q + a, 1), :] * same for a in range(5)], axis=0
                ).astype(jnp.bfloat16)
            )
        turned = [f32dot(block[:, :80], turn_ref[...]).astype(jnp.bfloat16) for block in blocks]
        for q, block, bubble in zip(batch, blocks, bubbles):
            left = f32dot(bubble[:, :80], block)
            for a in range(5):
                left_ref[pl.ds(80 * q + a, 16, stride=5), :] = left[16 * a : 16 * a + 16]
        for q, bubble, matrix in zip(batch, bubbles, turned):
            right_ref[q] = f32dot(matrix[:, :80], bubble).astype(jnp.bfloat16)


def finish_part(part, got_ref, split_ref, spread_ref):
    rows = jnp.concatenate(
        [got_ref[8 * (4 * part + g) : 8 * (4 * part + g) + 8].reshape(192, 128) for g in range(4)], axis=1
    )
    apart = f32dot(rows, split_ref[...]).astype(jnp.bfloat16)
    for qx in range(QX):
        spread_ref[qx, :, 128 * part : 128 * part + 128] = apart[:, 128 * qx : 128 * qx + 128]


def finish(gather_ref, spread_ref, blocks_ref, left_ref, right_ref, rows_ref, out_ref):
    for qx in range(QX):
        found = f32dot(spread_ref[qx], gather_ref[...])
        for a in range(5):
            blocks_ref[a, 192 * qx : 192 * qx + 192, :] = found[:, 128 * a : 128 * a + 128]

    for q in range(QX * QY):
        at = q + 182 * (q // 10)
        block = jnp.concatenate(
            [blocks_ref[a, pl.ds(at, 16, stride=12), :] for a in range(5)], axis=0
        ).astype(jnp.bfloat16)
        left = left_ref[80 * q : 80 * q + 80, :].astype(jnp.bfloat16)
        result = f32dot(block[:, :80], left) + f32dot(right_ref[q][:, :80], block)
        put = q + 6 * (q // 10)
        for a in range(5):
            rows_ref[pl.ds(80 * a + put, 16, stride=400), :] = result[16 * a : 16 * a + 16]

    for qx in range(QX):
        for i in range(0, ORDER, 8):
            wide = jnp.concatenate(
                [rows_ref[80 * (i + k) + 16 * qx : 80 * (i + k) + 16 * qx + 16, :80] for k in range(8)], axis=1
            ).astype(jnp.bfloat16)
            out_ref[qx, :, 80 * i : 80 * i + 640] = wide[:10]


def main_kernel(
    pair_ref, shift_ref, envelope_ref, xb_ref, yb_ref, turn_ref, same_ref,
    crossed_hbm, spread_hbm, merge_hbm, vertex_hbm, bubble_hbm, yf_hbm, cas_hbm, split_hbm, gather_hbm,
    out_ref,
    crossed_ref, spread_ref, merge_ref, vertex_ref, bubble_ref, yf_ref, cas_ref, split_ref, gather_ref,
    mixed_ref, slabs_ref, recv_ref, half_ref, back_ref, outgoing_ref, got_ref, weight_ref,
    vertex_rows_ref, wide_ref, lines_ref, left_ref, right_ref, spread_back_ref, blocks_ref, out_rows_ref,
    load_sems, send_sem, recv_sems, back_send_sem, back_sems,
):
    sources = (crossed_hbm, spread_hbm, merge_hbm, vertex_hbm, bubble_hbm, yf_hbm, cas_hbm, split_hbm, gather_hbm)
    places = (crossed_ref, spread_ref, merge_ref, vertex_ref, bubble_ref, yf_ref, cas_ref, split_ref, gather_ref)
    loads = [
        pltpu.make_async_copy(source, place, load_sems.at[k])
        for k, (source, place) in enumerate(zip(sources, places))
    ]
    for load in loads:
        load.start()
    mx = lax.axis_index("kx")
    my = lax.axis_index("ky")
    me = mx * NY + my
    barrier = pltpu.get_barrier_semaphore()

    def partner(step):
        other = lax.rem(me + lax.rem(step * 37, DEVICES), DEVICES)
        return other, (other // NY, lax.rem(other, NY))

    def greet(step, carry):
        _, where = partner(step)
        pl.semaphore_signal(barrier, inc=1, device_id=where, device_id_type=MESH)
        return carry

    lax.fori_loop(1, DEVICES, greet, 0)
    for load in loads[:3]:
        load.wait()
    build_slabs(crossed_ref, spread_ref, merge_ref, mixed_ref, slabs_ref)
    own = pltpu.make_async_copy(slabs_ref.at[me], recv_ref.at[me], recv_sems.at[mx])
    own.start()
    pl.semaphore_wait(barrier, DEVICES - 1)

    def send(step, carry):
        other, where = partner(step)
        pltpu.make_async_remote_copy(
            src_ref=slabs_ref.at[other],
            dst_ref=recv_ref.at[me],
            send_sem=send_sem,
            recv_sem=recv_sems.at[mx],
            device_id=where,
            device_id_type=MESH,
        ).start()
        return carry

    lax.fori_loop(1, DEVICES, send, 0, unroll=True)
    weight_ref[...] = jnp.zeros_like(weight_ref)
    weight_ref[:, :, :LAT] = envelope_ref[...]
    for load in loads[3:]:
        load.wait()
    prepare_vertex(
        vertex_ref, bubble_ref, turn_ref, same_ref, vertex_rows_ref, wide_ref, lines_ref, left_ref, right_ref
    )

    for group in range(NX):
        here = pl.ds(NY * group, NY)
        pltpu.make_async_copy(slabs_ref.at[here], recv_ref.at[here], recv_sems.at[group]).wait()
        block = recv_ref[here].reshape(NY * SEND_ROWS, 128)
        turned = f32dot(block, yf_ref[...], ((0,), (0,)))
        for part in range(4):
            half_ref[part, 125 * group : 125 * group + 125, :] = turned[:125, 128 * part : 128 * part + 128]

    reals = []
    for pair in range(25):
        for chan in range(2):
            rows = pl.ds(pair_ref[chan, pair], LAT, stride=25)
            operand = jnp.concatenate(
                [half_ref[2 * chan + half, rows, :] for half in range(2)], axis=1
            ).astype(jnp.bfloat16)
            step_x = shift_ref[chan, pair // 5, 0, pair % 5]
            reals.append(f32dot(cas_ref[step_x + REACH], operand))
    projected = []
    for pair in range(25):
        total = [None, None]
        for chan in range(2):
            step_y = shift_ref[chan, pair // 5, 1, pair % 5]
            for half in range(2):
                piece = reals[2 * pair + chan][:, 128 * half : 128 * half + 128]
                term = pltpu.roll(piece, 128 - REACH - step_y, 1) * weight_ref[chan]
                total[half] = term if chan == 0 else total[half] + term
        projected.append(jnp.concatenate(total, axis=1).astype(jnp.bfloat16))
    for pair in range(25):
        back = f32dot(xb_ref[...], projected[pair])
        for half in range(2):
            back_ref[half, pl.ds(pair, 128, stride=25), :] = back[:, 128 * half : 128 * half + 128]

    for step in range(NX):
        group = lax.rem(mx + step, NX)
        rows = pl.ds(pl.multiple_of(200 * group, 8), 128)
        operand = jnp.concatenate(
            [back_ref[half, rows, :] for half in range(2)], axis=1
        ).astype(jnp.bfloat16)
        result = f32dot(yb_ref[...], operand, ((1,), (1,))).astype(jnp.bfloat16)
        for lane in range(NY):
            outgoing_ref[NY * group + lane] = result[BACK_ROWS * lane : BACK_ROWS * lane + BACK_ROWS]
        for turn in range(NY):
            lane = lax.rem(my + turn, NY)
            if step == 0 and turn == 0:
                pltpu.make_async_copy(outgoing_ref.at[me], got_ref.at[me], back_sems.at[mx // 4]).start()
            else:
                pltpu.make_async_remote_copy(
                    src_ref=outgoing_ref.at[NY * group + lane],
                    dst_ref=got_ref.at[me],
                    send_sem=back_send_sem,
                    recv_sem=back_sems.at[mx // 4],
                    device_id=(group, lane),
                    device_id_type=MESH,
                ).start()

    most = pl.ds(0, DEVICES - 1)
    pltpu.make_async_copy(slabs_ref.at[most], recv_ref.at[most], send_sem).wait()
    for part in range(4):
        here = pl.ds(32 * part, 32)
        pltpu.make_async_copy(outgoing_ref.at[here], got_ref.at[here], back_sems.at[part]).wait()
        finish_part(part, got_ref, split_ref, spread_back_ref)
    finish(gather_ref, spread_back_ref, blocks_ref, left_ref, right_ref, out_rows_ref, out_ref)
    pltpu.make_async_copy(outgoing_ref.at[most], got_ref.at[most], back_send_sem).wait()


def local(crossed, vertex, bubble, pair_map, bond_shift, envelope):
    f32 = jnp.float32
    bf16 = jnp.bfloat16
    crossed = crossed.transpose(1, 2, 0, 3).reshape(QX * QY, 2, ORDER * ORDER)
    bubble = bubble.transpose(0, 1, 3, 4, 2).reshape(QX * QY, NFF, NFF, NFREQ)
    bond_shift = bond_shift.transpose(0, 1, 3, 2)
    small = [x_back(), y_back(), turn_columns(), same_frequency()]
    small = [jnp.asarray(table) for table in small]
    large = [
        crossed, jnp.asarray(spread_source()), jnp.asarray(merge_x()), vertex, bubble,
        jnp.asarray(y_forward()), jnp.asarray(rolled_rows()), jnp.asarray(split_x()), jnp.asarray(gather_rows()),
    ]
    smem = pl.BlockSpec(memory_space=pltpu.SMEM)
    vmem = pl.BlockSpec(memory_space=pltpu.VMEM)
    hbm = pl.BlockSpec(memory_space=pl.ANY)
    return pl.pallas_call(
        main_kernel,
        out_shape=jax.ShapeDtypeStruct(vertex.shape, bf16),
        in_specs=[smem, smem, vmem] + [vmem] * len(small) + [hbm] * len(large),
        out_specs=vmem,
        scratch_shapes=[pltpu.VMEM(array.shape, array.dtype) for array in large] + [
            pltpu.VMEM((4, QX, 20 * NFREQ, 128), f32),
            pltpu.VMEM((DEVICES, SEND_ROWS, 128), bf16),
            pltpu.VMEM((DEVICES, SEND_ROWS, 128), bf16),
            pltpu.VMEM((4, 25 * LAT, 128), f32),
            pltpu.VMEM((2, 25 * NX * 8, 128), f32),
            pltpu.VMEM((DEVICES, BACK_ROWS, 128), bf16),
            pltpu.VMEM((DEVICES, BACK_ROWS, 128), bf16),
            pltpu.VMEM((2, LAT, 128), f32),
            pltpu.VMEM((80 * ORDER, 128), f32),
            pltpu.VMEM((250, 8, 128), f32),
            pltpu.VMEM((250, 128), f32),
            pltpu.VMEM((QX * QY * ORDER, 128), f32),
            pltpu.VMEM((QX * QY, ORDER, 128), bf16),
            pltpu.VMEM((QX, 192, 512), bf16),
            pltpu.VMEM((5, 192 * QX, 128), f32),
            pltpu.VMEM((80 * ORDER, 128), f32),
            pltpu.SemaphoreType.DMA((len(large),)),
            pltpu.SemaphoreType.DMA,
            pltpu.SemaphoreType.DMA((NX,)),
            pltpu.SemaphoreType.DMA,
            pltpu.SemaphoreType.DMA((4,)),
        ],
        compiler_params=pltpu.CompilerParams(
            collective_id=0, has_side_effects=True, vmem_limit_bytes=60 * 2**20
        ),
    )(pair_map, bond_shift, envelope, *small, *large)


def solution(mesh):
    placed = (
        P(None, "kx", "ky", None),
        P("kx", "ky", None),
        P("kx", "ky", None, None, None),
        P(),
        P(),
        P(),
    )
    return jax.shard_map(
        local, mesh=mesh, in_specs=placed, out_specs=P("kx", "ky", None), check_vma=False
    )
```

```python
import math

import jax
import jax.numpy as jnp
import ml_dtypes
import numpy as np
from jax import lax
from jax.experimental import pallas as pl
from jax.experimental.pallas import tpu as pltpu
from jax.sharding import PartitionSpec as P

LAT = 80
NFF = 5
NFREQ = 16
ORDER = 80
NX = 16
NY = 8
DEVICES = NX * NY
QX = LAT // NX
QY = LAT // NY
REACH = 2
SEND_ROWS = 40
BACK_ROWS = 24
BATCH = 25
BF16 = ml_dtypes.bfloat16
MESH = pl.DeviceIdType.MESH


def cas_table(count):
    phases = np.outer(np.arange(count), np.arange(count)) % count
    angles = phases * (2.0 * math.pi / count)
    return ((np.cos(angles) + np.sin(angles)) / math.sqrt(count)).astype(np.float32)


CAS = cas_table(LAT)


def rolled_rows():
    rows = (np.arange(LAT)[None, :] + np.arange(-REACH, REACH + 1)[:, None]) % LAT
    return CAS[rows].astype(BF16)


def y_forward():
    reach = np.zeros((LAT, 128), np.float32)
    columns = np.arange(LAT + 2 * REACH)
    reach[:, columns] = CAS[:, (columns - REACH) % LAT]
    reach = reach.reshape(NY, QY, 128)
    table = np.zeros((NY, 2, QY, 2, 2, 2, 128), np.float32)
    for chan in range(2):
        for half in range(2):
            table[:, half, :, chan, chan, half] = reach
    return table.reshape(NY * SEND_ROWS, 4 * 128).astype(BF16)


def x_back():
    table = np.zeros((NX, 8, LAT), np.float32)
    table[:, :QX] = CAS.reshape(NX, QX, LAT)
    return table.reshape(NX * 8, LAT).astype(BF16)


def y_back():
    table = np.zeros((NY, 2, 12, 2, 128), np.float32)
    for half in range(2):
        table[:, half, :QY, half, :LAT] = CAS.reshape(NY, QY, LAT)
    return table.reshape(NY * BACK_ROWS, 2 * 128).astype(BF16)


def spread_source():
    table = np.zeros((112 + 400 + 112, 16 * 32), np.float32)
    a, n2, b = np.meshgrid(np.arange(5), np.arange(16), np.arange(5), indexing="ij")
    table[112 + 80 * a + 5 * n2 + b, 32 * n2 + 5 * a + b] = 1
    return table.astype(BF16)


def merge_x():
    table = np.zeros((5, 4, 32, 4, 128), np.float32)
    qx, g, pair = np.meshgrid(np.arange(5), np.arange(4), np.arange(25), indexing="ij")
    table[qx, g, pair, g, 25 * qx + pair] = 1
    return table.reshape(640, 512).astype(BF16)


def split_x():
    return np.ascontiguousarray(merge_x().T)


def gather_rows():
    table = np.zeros((16, 32, 5, 128), np.float32)
    a, n2, b = np.meshgrid(np.arange(5), np.arange(16), np.arange(5), indexing="ij")
    table[n2, 5 * a + b, a, 5 * n2 + b] = 1
    return table.reshape(512, 640).astype(BF16)


def turn_columns():
    table = np.zeros((80, 128), np.float32)
    n, a = np.meshgrid(np.arange(16), np.arange(5), indexing="ij")
    table[5 * n + a, 16 * a + n] = 1
    return table.astype(BF16)


def same_frequency():
    table = np.zeros((16, 128), np.float32)
    n, b = np.meshgrid(np.arange(16), np.arange(5), indexing="ij")
    table[n, 16 * b + n] = 1
    return table


def partner_order():
    offsets = [(z, y, x, c) for z in range(4) for y in range(4) for x in range(4) for c in range(2)]
    links = [sum(min(step, 4 - step) for step in offset[:3]) for offset in offsets]
    ranked = sorted(zip(links, offsets), key=lambda pair: -pair[0])
    return [offset for _, offset in ranked if offset != (0, 0, 0, 0)]


def partners(mx, my):
    mz, my_y = mx // 4, my // 2
    mine_x = lax.rem(my, 2) * 2 + lax.rem(mx // 2, 2)
    mine_core = lax.rem(mx, 2)
    for z, y, x, core in partner_order():
        there = lax.rem(mine_x + x, 4)
        kx = lax.rem(mz + z, 4) * 4 + lax.rem(there, 2) * 2 + lax.rem(mine_core + core, 2)
        ky = lax.rem(my_y + y, 4) * 2 + there // 2
        yield kx, ky


def f32dot(left, right, dims=((1,), (0,))):
    return lax.dot_general(left, right, (dims, ((), ())), preferred_element_type=jnp.float32)


def build_slabs(crossed_ref, spread_ref, merge_ref, mixed_ref, slabs_ref):
    for n in range(NFREQ):
        start = 400 * n // 128 * 128
        offset = 400 * n - start
        rows = crossed_ref[:, :, start : start + 512].reshape(2 * QX * QY, 512)
        spread = f32dot(rows, spread_ref[112 - offset : 624 - offset, :])
        for part in range(4):
            for qx in range(QX):
                mixed_ref[part, qx, 20 * n : 20 * n + 20, :] = spread[
                    20 * qx : 20 * qx + 20, 128 * part : 128 * part + 128
                ]

    def one_part(part, carry):
        rows = jnp.concatenate([mixed_ref[part, qx] for qx in range(QX)], axis=1).astype(jnp.bfloat16)
        merged = f32dot(rows, merge_ref[...]).astype(jnp.bfloat16)
        for g in range(4):
            for pair in range(8):
                slabs_ref[(4 * part + g) * 8 + pair] = merged[
                    40 * pair : 40 * pair + 40, 128 * g : 128 * g + 128
                ]
        return carry

    for part in range(4):
        one_part(part, 0)


def prepare_vertex(
    vertex_ref, bubble_ref, turn_ref, same_ref, rows_ref, wide_ref, lines_ref, left_ref, right_ref
):
    for qx in range(QX):
        for i in range(ORDER):
            rows_ref[80 * i + 16 * qx : 80 * i + 16 * qx + 10, :80] = vertex_ref[
                qx, :, 80 * i : 80 * i + 80
            ].astype(jnp.float32)
    same = same_ref[...]
    wide_ref[:, :5, :16] = bubble_ref[...].reshape(250, 5, 16).astype(jnp.float32)
    lines_ref[:, :80] = jnp.concatenate([wide_ref[:, b, :16] for b in range(5)], axis=1)

    for start in range(0, QX * QY, BATCH):
        batch = range(start, start + BATCH)
        blocks = []
        bubbles = []
        for q in batch:
            at = q + 6 * (q // 10)
            blocks.append(
                jnp.concatenate(
                    [rows_ref[pl.ds(80 * a + at, 16, stride=400), :] for a in range(5)], axis=0
                ).astype(jnp.bfloat16)
            )
            bubbles.append(
                jnp.concatenate(
                    [lines_ref[pl.ds(5 * q + a, 1), :] * same for a in range(5)], axis=0
                ).astype(jnp.bfloat16)
            )
        turned = [f32dot(block[:, :80], turn_ref[...]).astype(jnp.bfloat16) for block in blocks]
        for q, block, bubble in zip(batch, blocks, bubbles):
            left = f32dot(bubble[:, :80], block)
            for a in range(5):
                left_ref[pl.ds(80 * q + a, 16, stride=5), :] = left[16 * a : 16 * a + 16]
        for q, bubble, matrix in zip(batch, bubbles, turned):
            right_ref[q] = f32dot(matrix[:, :80], bubble).astype(jnp.bfloat16)


def finish_part(part, got_ref, split_ref, spread_ref):
    rows = jnp.concatenate(
        [got_ref[8 * (4 * part + g) : 8 * (4 * part + g) + 8].reshape(192, 128) for g in range(4)], axis=1
    )
    apart = f32dot(rows, split_ref[...]).astype(jnp.bfloat16)
    for qx in range(QX):
        spread_ref[qx, :, 128 * part : 128 * part + 128] = apart[:, 128 * qx : 128 * qx + 128]


def finish(gather_ref, spread_ref, blocks_ref, left_ref, right_ref, rows_ref, out_ref):
    for qx in range(QX):
        found = f32dot(spread_ref[qx], gather_ref[...])
        for a in range(5):
            blocks_ref[a, 192 * qx : 192 * qx + 192, :] = found[:, 128 * a : 128 * a + 128]

    for q in range(QX * QY):
        at = q + 182 * (q // 10)
        block = jnp.concatenate(
            [blocks_ref[a, pl.ds(at, 16, stride=12), :] for a in range(5)], axis=0
        ).astype(jnp.bfloat16)
        left = left_ref[80 * q : 80 * q + 80, :].astype(jnp.bfloat16)
        result = f32dot(block[:, :80], left) + f32dot(right_ref[q][:, :80], block)
        put = q + 6 * (q // 10)
        for a in range(5):
            rows_ref[pl.ds(80 * a + put, 16, stride=400), :] = result[16 * a : 16 * a + 16]

    for qx in range(QX):
        for i in range(0, ORDER, 8):
            wide = jnp.concatenate(
                [rows_ref[80 * (i + k) + 16 * qx : 80 * (i + k) + 16 * qx + 16, :80] for k in range(8)], axis=1
            ).astype(jnp.bfloat16)
            out_ref[qx, :, 80 * i : 80 * i + 640] = wide[:10]


def main_kernel(*refs):
    (
        crossed_hbm, spread_hbm, merge_hbm, pair_hbm, shift_hbm, envelope_hbm, vertex_hbm, bubble_hbm, same_hbm,
        turn_hbm, yf_hbm, cas_hbm, xb_hbm, yb_hbm, split_hbm, gather_hbm,
        out_ref,
        crossed_ref, spread_ref, merge_ref, pair_ref, shift_ref, envelope_ref, vertex_ref, bubble_ref, same_ref,
        turn_ref, yf_ref, cas_ref, xb_ref, yb_ref, split_ref, gather_ref,
        mixed_ref, slabs_ref, recv_ref, half_ref, back_ref, outgoing_ref, got_ref, weight_ref,
        vertex_rows_ref, wide_ref, lines_ref, left_ref, right_ref, spread_back_ref, blocks_ref, out_rows_ref,
        load_sems, send_sem, recv_sems, back_send_sem, back_sems,
    ) = refs
    loads = [pltpu.make_async_copy(refs[k], refs[17 + k], load_sems.at[k]) for k in range(16)]
    for load in loads:
        load.start()
    mx = lax.axis_index("kx")
    my = lax.axis_index("ky")
    me = mx * NY + my
    barrier = pltpu.get_barrier_semaphore()

    for kx, ky in partners(mx, my):
        pl.semaphore_signal(barrier, inc=1, device_id=(kx, ky), device_id_type=MESH)
    for load in loads[:3]:
        load.wait()
    build_slabs(crossed_ref, spread_ref, merge_ref, mixed_ref, slabs_ref)
    own = pltpu.make_async_copy(slabs_ref.at[me], recv_ref.at[me], recv_sems.at[mx])
    own.start()
    pl.semaphore_wait(barrier, DEVICES - 1)

    for kx, ky in partners(mx, my):
        pltpu.make_async_remote_copy(
            src_ref=slabs_ref.at[kx * NY + ky],
            dst_ref=recv_ref.at[me],
            send_sem=send_sem,
            recv_sem=recv_sems.at[mx],
            device_id=(kx, ky),
            device_id_type=MESH,
        ).start()

    for load in loads[3:]:
        load.wait()
    weight_ref[...] = jnp.zeros_like(weight_ref)
    weight_ref[:, :, :LAT] = envelope_ref[...]
    prepare_vertex(
        vertex_ref, bubble_ref, turn_ref, same_ref, vertex_rows_ref, wide_ref, lines_ref, left_ref, right_ref
    )

    for group in range(NX):
        here = pl.ds(NY * group, NY)
        pltpu.make_async_copy(slabs_ref.at[here], recv_ref.at[here], recv_sems.at[group]).wait()
        block = recv_ref[here].reshape(NY * SEND_ROWS, 128)
        turned = f32dot(block, yf_ref[...], ((0,), (0,)))
        for part in range(4):
            half_ref[part, 125 * group : 125 * group + 125, :] = turned[:125, 128 * part : 128 * part + 128]

    reals = []
    for pair in range(25):
        for chan in range(2):
            rows = pl.ds(pair_ref[chan, pair], LAT, stride=25)
            operand = jnp.concatenate(
                [half_ref[2 * chan + half, rows, :] for half in range(2)], axis=1
            ).astype(jnp.bfloat16)
            step_x = shift_ref[chan, pair // 5, 0, pair % 5]
            reals.append(f32dot(cas_ref[step_x + REACH], operand))
    projected = []
    for pair in range(25):
        total = [None, None]
        for chan in range(2):
            step_y = shift_ref[chan, pair // 5, 1, pair % 5]
            for half in range(2):
                piece = reals[2 * pair + chan][:, 128 * half : 128 * half + 128]
                term = pltpu.roll(piece, 128 - REACH - step_y, 1) * weight_ref[chan]
                total[half] = term if chan == 0 else total[half] + term
        projected.append(jnp.concatenate(total, axis=1).astype(jnp.bfloat16))
    for pair in range(25):
        back = f32dot(xb_ref[...], projected[pair])
        for half in range(2):
            back_ref[half, pl.ds(pair, 128, stride=25), :] = back[:, 128 * half : 128 * half + 128]

    for group in range(NX):
        rows = pl.ds(200 * group, 128)
        operand = jnp.concatenate(
            [back_ref[half, rows, :] for half in range(2)], axis=1
        ).astype(jnp.bfloat16)
        result = f32dot(yb_ref[...], operand, ((1,), (1,))).astype(jnp.bfloat16)
        for lane in range(NY):
            outgoing_ref[NY * group + lane] = result[BACK_ROWS * lane : BACK_ROWS * lane + BACK_ROWS]
    pltpu.make_async_copy(outgoing_ref.at[me], got_ref.at[me], back_sems.at[mx // 4]).start()
    for kx, ky in partners(mx, my):
        pltpu.make_async_remote_copy(
            src_ref=outgoing_ref.at[kx * NY + ky],
            dst_ref=got_ref.at[me],
            send_sem=back_send_sem,
            recv_sem=back_sems.at[mx // 4],
            device_id=(kx, ky),
            device_id_type=MESH,
        ).start()

    most = pl.ds(0, DEVICES - 1)
    pltpu.make_async_copy(slabs_ref.at[most], recv_ref.at[most], send_sem).wait()
    for part in range(4):
        here = pl.ds(32 * part, 32)
        pltpu.make_async_copy(outgoing_ref.at[here], got_ref.at[here], back_sems.at[part]).wait()
        finish_part(part, got_ref, split_ref, spread_back_ref)
    finish(gather_ref, spread_back_ref, blocks_ref, left_ref, right_ref, out_rows_ref, out_ref)
    pltpu.make_async_copy(outgoing_ref.at[most], got_ref.at[most], back_send_sem).wait()


def local(crossed, vertex, bubble, pair_map, bond_shift, envelope):
    f32 = jnp.float32
    bf16 = jnp.bfloat16
    crossed = crossed.transpose(1, 2, 0, 3).reshape(QX * QY, 2, ORDER * ORDER)
    bubble = bubble.transpose(0, 1, 3, 4, 2).reshape(QX * QY, NFF, NFF, NFREQ)
    bond_shift = bond_shift.transpose(0, 1, 3, 2)
    operands = [
        crossed, spread_source(), merge_x(), pair_map, bond_shift, envelope, vertex, bubble, same_frequency(),
        turn_columns(), y_forward(), rolled_rows(), x_back(), y_back(), split_x(), gather_rows(),
    ]
    operands = [jnp.asarray(operand) for operand in operands]
    hbm = pl.BlockSpec(memory_space=pl.ANY)
    result = pl.pallas_call(
        main_kernel,
        out_shape=jax.ShapeDtypeStruct(vertex.shape, bf16),
        in_specs=[hbm] * len(operands),
        out_specs=pl.BlockSpec(memory_space=pltpu.VMEM),
        scratch_shapes=[
            (pltpu.SMEM if array.dtype == jnp.int32 else pltpu.VMEM)(array.shape, array.dtype)
            for array in operands
        ] + [
            pltpu.VMEM((4, QX, 20 * NFREQ, 128), f32),
            pltpu.VMEM((DEVICES, SEND_ROWS, 128), bf16),
            pltpu.VMEM((DEVICES, SEND_ROWS, 128), bf16),
            pltpu.VMEM((4, 25 * LAT, 128), f32),
            pltpu.VMEM((2, 25 * NX * 8, 128), f32),
            pltpu.VMEM((DEVICES, BACK_ROWS, 128), bf16),
            pltpu.VMEM((DEVICES, BACK_ROWS, 128), bf16),
            pltpu.VMEM((2, LAT, 128), f32),
            pltpu.VMEM((80 * ORDER, 128), f32),
            pltpu.VMEM((250, 8, 128), f32),
            pltpu.VMEM((250, 128), f32),
            pltpu.VMEM((QX * QY * ORDER, 128), f32),
            pltpu.VMEM((QX * QY, ORDER, 128), bf16),
            pltpu.VMEM((QX, 192, 512), bf16),
            pltpu.VMEM((5, 192 * QX, 128), f32),
            pltpu.VMEM((80 * ORDER, 128), f32),
            pltpu.SemaphoreType.DMA((len(operands),)),
            pltpu.SemaphoreType.DMA,
            pltpu.SemaphoreType.DMA((NX,)),
            pltpu.SemaphoreType.DMA,
            pltpu.SemaphoreType.DMA((4,)),
        ],
        compiler_params=pltpu.CompilerParams(
            collective_id=0, has_side_effects=True, vmem_limit_bytes=60 * 2**20
        ),
    )(*operands)
    return result


def solution(mesh):
    placed = (
        P(None, "kx", "ky", None),
        P("kx", "ky", None),
        P("kx", "ky", None, None, None),
        P(),
        P(),
        P(),
    )
    return jax.shard_map(
        local, mesh=mesh, in_specs=placed, out_specs=P("kx", "ky", None), check_vma=False
    )
```

```python
import math

import jax
import jax.numpy as jnp
import ml_dtypes
import numpy as np
from jax import lax
from jax.experimental import pallas as pl
from jax.experimental.pallas import tpu as pltpu
from jax.sharding import PartitionSpec as P

LAT = 80
NFF = 5
NFREQ = 16
ORDER = 80
NX = 16
NY = 8
DEVICES = NX * NY
QX = LAT // NX
QY = LAT // NY
REACH = 2
SEND_ROWS = 40
BACK_ROWS = 24
BATCH = 25
BF16 = ml_dtypes.bfloat16
MESH = pl.DeviceIdType.MESH


def cas_table(count):
    phases = np.outer(np.arange(count), np.arange(count)) % count
    angles = phases * (2.0 * math.pi / count)
    return ((np.cos(angles) + np.sin(angles)) / math.sqrt(count)).astype(np.float32)


CAS = cas_table(LAT)


def rolled_rows():
    rows = (np.arange(LAT)[None, :] + np.arange(-REACH, REACH + 1)[:, None]) % LAT
    return CAS[rows].astype(BF16)


def y_forward():
    reach = np.zeros((LAT, 128), np.float32)
    columns = np.arange(LAT + 2 * REACH)
    reach[:, columns] = CAS[:, (columns - REACH) % LAT]
    reach = reach.reshape(NY, QY, 128)
    table = np.zeros((NY, 2, QY, 2, 2, 2, 128), np.float32)
    for chan in range(2):
        for half in range(2):
            table[:, half, :, chan, chan, half] = reach
    return table.reshape(NY * SEND_ROWS, 4 * 128).astype(BF16)


def x_back():
    table = np.zeros((NX, 8, LAT), np.float32)
    table[:, :QX] = CAS.reshape(NX, QX, LAT)
    return table.reshape(NX * 8, LAT).astype(BF16)


def y_back():
    table = np.zeros((NY, 2, 12, 2, 128), np.float32)
    for half in range(2):
        table[:, half, :QY, half, :LAT] = CAS.reshape(NY, QY, LAT)
    return table.reshape(NY * BACK_ROWS, 2 * 128).astype(BF16)


def spread_source():
    table = np.zeros((112 + 400 + 112, 16 * 32), np.float32)
    a, n2, b = np.meshgrid(np.arange(5), np.arange(16), np.arange(5), indexing="ij")
    table[112 + 80 * a + 5 * n2 + b, 32 * n2 + 5 * a + b] = 1
    return table.astype(BF16)


def merge_x():
    table = np.zeros((5, 4, 32, 4, 128), np.float32)
    qx, g, pair = np.meshgrid(np.arange(5), np.arange(4), np.arange(25), indexing="ij")
    table[qx, g, pair, g, 25 * qx + pair] = 1
    return table.reshape(640, 512).astype(BF16)


def split_x():
    return np.ascontiguousarray(merge_x().T)


def gather_rows():
    table = np.zeros((16, 32, 5, 128), np.float32)
    a, n2, b = np.meshgrid(np.arange(5), np.arange(16), np.arange(5), indexing="ij")
    table[n2, 5 * a + b, a, 5 * n2 + b] = 1
    return table.reshape(512, 640).astype(BF16)


def turn_columns():
    table = np.zeros((80, 128), np.float32)
    n, a = np.meshgrid(np.arange(16), np.arange(5), indexing="ij")
    table[5 * n + a, 16 * a + n] = 1
    return table.astype(BF16)


def same_frequency():
    table = np.zeros((16, 128), np.float32)
    n, b = np.meshgrid(np.arange(16), np.arange(5), indexing="ij")
    table[n, 16 * b + n] = 1
    return table


def partner_order():
    offsets = [(z, y, x, c) for z in range(4) for y in range(4) for x in range(4) for c in range(2)]
    offsets = [offset for offset in offsets if offset != (0, 0, 0, 0)]
    draw = np.random.RandomState(1).permutation(len(offsets))
    links = [sum(min(step, 4 - step) for step in offset[:3]) for offset in offsets]
    return [offsets[k] for k in sorted(range(len(offsets)), key=lambda k: (-links[k], draw[k]))]


def partners(mx, my):
    mz, my_y = mx // 4, my // 2
    mine_x = lax.rem(my, 2) * 2 + lax.rem(mx // 2, 2)
    mine_core = lax.rem(mx, 2)
    for z, y, x, core in partner_order():
        there = lax.rem(mine_x + x, 4)
        kx = lax.rem(mz + z, 4) * 4 + lax.rem(there, 2) * 2 + lax.rem(mine_core + core, 2)
        ky = lax.rem(my_y + y, 4) * 2 + there // 2
        yield kx, ky


def f32dot(left, right, dims=((1,), (0,))):
    return lax.dot_general(left, right, (dims, ((), ())), preferred_element_type=jnp.float32)


def build_slabs(crossed_ref, spread_ref, merge_ref, mixed_ref, slabs_ref):
    for n in range(NFREQ):
        start = 400 * n // 128 * 128
        offset = 400 * n - start
        rows = crossed_ref[:, :, start : start + 512].reshape(2 * QX * QY, 512)
        spread = f32dot(rows, spread_ref[112 - offset : 624 - offset, :])
        for part in range(4):
            for qx in range(QX):
                mixed_ref[part, qx, 20 * n : 20 * n + 20, :] = spread[
                    20 * qx : 20 * qx + 20, 128 * part : 128 * part + 128
                ]

    def one_part(part, carry):
        rows = jnp.concatenate([mixed_ref[part, qx] for qx in range(QX)], axis=1).astype(jnp.bfloat16)
        merged = f32dot(rows, merge_ref[...]).astype(jnp.bfloat16)
        for g in range(4):
            for pair in range(8):
                slabs_ref[(4 * part + g) * 8 + pair] = merged[
                    40 * pair : 40 * pair + 40, 128 * g : 128 * g + 128
                ]
        return carry

    for part in range(4):
        one_part(part, 0)


def prepare_vertex(
    vertex_ref, bubble_ref, turn_ref, same_ref, rows_ref, wide_ref, lines_ref, left_ref, right_ref
):
    for qx in range(QX):
        for i in range(ORDER):
            rows_ref[80 * i + 16 * qx : 80 * i + 16 * qx + 10, :80] = vertex_ref[
                qx, :, 80 * i : 80 * i + 80
            ].astype(jnp.float32)
    same = same_ref[...]
    wide_ref[:, :5, :16] = bubble_ref[...].reshape(250, 5, 16).astype(jnp.float32)
    lines_ref[:, :80] = jnp.concatenate([wide_ref[:, b, :16] for b in range(5)], axis=1)

    for start in range(0, QX * QY, BATCH):
        batch = range(start, start + BATCH)
        blocks = []
        bubbles = []
        for q in batch:
            at = q + 6 * (q // 10)
            blocks.append(
                jnp.concatenate(
                    [rows_ref[pl.ds(80 * a + at, 16, stride=400), :] for a in range(5)], axis=0
                ).astype(jnp.bfloat16)
            )
            bubbles.append(
                jnp.concatenate(
                    [lines_ref[pl.ds(5 * q + a, 1), :] * same for a in range(5)], axis=0
                ).astype(jnp.bfloat16)
            )
        turned = [f32dot(block[:, :80], turn_ref[...]).astype(jnp.bfloat16) for block in blocks]
        for q, block, bubble in zip(batch, blocks, bubbles):
            left = f32dot(bubble[:, :80], block)
            for a in range(5):
                left_ref[pl.ds(80 * q + a, 16, stride=5), :] = left[16 * a : 16 * a + 16]
        for q, bubble, matrix in zip(batch, bubbles, turned):
            right_ref[q] = f32dot(matrix[:, :80], bubble).astype(jnp.bfloat16)


def finish_part(part, got_ref, split_ref, spread_ref):
    rows = jnp.concatenate(
        [got_ref[8 * (4 * part + g) : 8 * (4 * part + g) + 8].reshape(192, 128) for g in range(4)], axis=1
    )
    apart = f32dot(rows, split_ref[...]).astype(jnp.bfloat16)
    for qx in range(QX):
        spread_ref[qx, :, 128 * part : 128 * part + 128] = apart[:, 128 * qx : 128 * qx + 128]


def finish(gather_ref, spread_ref, blocks_ref, left_ref, right_ref, rows_ref, out_ref):
    for qx in range(QX):
        found = f32dot(spread_ref[qx], gather_ref[...])
        for a in range(5):
            blocks_ref[a, 192 * qx : 192 * qx + 192, :] = found[:, 128 * a : 128 * a + 128]

    for q in range(QX * QY):
        at = q + 182 * (q // 10)
        block = jnp.concatenate(
            [blocks_ref[a, pl.ds(at, 16, stride=12), :] for a in range(5)], axis=0
        ).astype(jnp.bfloat16)
        left = left_ref[80 * q : 80 * q + 80, :].astype(jnp.bfloat16)
        result = f32dot(block[:, :80], left) + f32dot(right_ref[q][:, :80], block)
        put = q + 6 * (q // 10)
        for a in range(5):
            rows_ref[pl.ds(80 * a + put, 16, stride=400), :] = result[16 * a : 16 * a + 16]

    for qx in range(QX):
        for i in range(0, ORDER, 8):
            wide = jnp.concatenate(
                [rows_ref[80 * (i + k) + 16 * qx : 80 * (i + k) + 16 * qx + 16, :80] for k in range(8)], axis=1
            ).astype(jnp.bfloat16)
            out_ref[qx, :, 80 * i : 80 * i + 640] = wide[:10]


def main_kernel(*refs):
    (
        crossed_hbm, spread_hbm, merge_hbm, pair_hbm, shift_hbm, envelope_hbm, vertex_hbm, bubble_hbm, same_hbm,
        turn_hbm, yf_hbm, cas_hbm, xb_hbm, yb_hbm, split_hbm, gather_hbm,
        out_ref,
        crossed_ref, spread_ref, merge_ref, pair_ref, shift_ref, envelope_ref, vertex_ref, bubble_ref, same_ref,
        turn_ref, yf_ref, cas_ref, xb_ref, yb_ref, split_ref, gather_ref,
        mixed_ref, slabs_ref, recv_ref, half_ref, back_ref, outgoing_ref, got_ref, weight_ref,
        vertex_rows_ref, wide_ref, lines_ref, left_ref, right_ref, spread_back_ref, blocks_ref, out_rows_ref,
        load_sems, send_sem, recv_sems, back_send_sem, back_sems,
    ) = refs
    loads = [pltpu.make_async_copy(refs[k], refs[17 + k], load_sems.at[k]) for k in range(16)]
    for load in loads:
        load.start()
    mx = lax.axis_index("kx")
    my = lax.axis_index("ky")
    me = mx * NY + my
    barrier = pltpu.get_barrier_semaphore()

    for kx, ky in partners(mx, my):
        pl.semaphore_signal(barrier, inc=1, device_id=(kx, ky), device_id_type=MESH)
    for load in loads[:3]:
        load.wait()
    build_slabs(crossed_ref, spread_ref, merge_ref, mixed_ref, slabs_ref)
    own = pltpu.make_async_copy(slabs_ref.at[me], recv_ref.at[me], recv_sems.at[mx])
    own.start()
    pl.semaphore_wait(barrier, DEVICES - 1)

    for kx, ky in partners(mx, my):
        pltpu.make_async_remote_copy(
            src_ref=slabs_ref.at[kx * NY + ky],
            dst_ref=recv_ref.at[me],
            send_sem=send_sem,
            recv_sem=recv_sems.at[mx],
            device_id=(kx, ky),
            device_id_type=MESH,
        ).start()

    for load in loads[3:]:
        load.wait()
    weight_ref[...] = jnp.zeros_like(weight_ref)
    weight_ref[:, :, :LAT] = envelope_ref[...]
    prepare_vertex(
        vertex_ref, bubble_ref, turn_ref, same_ref, vertex_rows_ref, wide_ref, lines_ref, left_ref, right_ref
    )

    for group in range(NX):
        here = pl.ds(NY * group, NY)
        pltpu.make_async_copy(slabs_ref.at[here], recv_ref.at[here], recv_sems.at[group]).wait()
        block = recv_ref[here].reshape(NY * SEND_ROWS, 128)
        turned = f32dot(block, yf_ref[...], ((0,), (0,)))
        for part in range(4):
            half_ref[part, 125 * group : 125 * group + 125, :] = turned[:125, 128 * part : 128 * part + 128]

    reals = []
    for pair in range(25):
        for chan in range(2):
            rows = pl.ds(pair_ref[chan, pair], LAT, stride=25)
            operand = jnp.concatenate(
                [half_ref[2 * chan + half, rows, :] for half in range(2)], axis=1
            ).astype(jnp.bfloat16)
            step_x = shift_ref[chan, pair // 5, 0, pair % 5]
            reals.append(f32dot(cas_ref[step_x + REACH], operand))
    projected = []
    for pair in range(25):
        total = [None, None]
        for chan in range(2):
            step_y = shift_ref[chan, pair // 5, 1, pair % 5]
            for half in range(2):
                piece = reals[2 * pair + chan][:, 128 * half : 128 * half + 128]
                term = pltpu.roll(piece, 128 - REACH - step_y, 1) * weight_ref[chan]
                total[half] = term if chan == 0 else total[half] + term
        projected.append(jnp.concatenate(total, axis=1).astype(jnp.bfloat16))
    for pair in range(25):
        back = f32dot(xb_ref[...], projected[pair])
        for half in range(2):
            back_ref[half, pl.ds(pair, 128, stride=25), :] = back[:, 128 * half : 128 * half + 128]

    for group in range(NX):
        rows = pl.ds(200 * group, 128)
        operand = jnp.concatenate(
            [back_ref[half, rows, :] for half in range(2)], axis=1
        ).astype(jnp.bfloat16)
        result = f32dot(yb_ref[...], operand, ((1,), (1,))).astype(jnp.bfloat16)
        for lane in range(NY):
            outgoing_ref[NY * group + lane] = result[BACK_ROWS * lane : BACK_ROWS * lane + BACK_ROWS]
    pltpu.make_async_copy(outgoing_ref.at[me], got_ref.at[me], back_sems.at[mx // 4]).start()
    for kx, ky in partners(mx, my):
        pltpu.make_async_remote_copy(
            src_ref=outgoing_ref.at[kx * NY + ky],
            dst_ref=got_ref.at[me],
            send_sem=back_send_sem,
            recv_sem=back_sems.at[mx // 4],
            device_id=(kx, ky),
            device_id_type=MESH,
        ).start()

    most = pl.ds(0, DEVICES - 1)
    pltpu.make_async_copy(slabs_ref.at[most], recv_ref.at[most], send_sem).wait()
    for part in range(4):
        here = pl.ds(32 * part, 32)
        pltpu.make_async_copy(outgoing_ref.at[here], got_ref.at[here], back_sems.at[part]).wait()
        finish_part(part, got_ref, split_ref, spread_back_ref)
    finish(gather_ref, spread_back_ref, blocks_ref, left_ref, right_ref, out_rows_ref, out_ref)
    pltpu.make_async_copy(outgoing_ref.at[most], got_ref.at[most], back_send_sem).wait()


def local(crossed, vertex, bubble, pair_map, bond_shift, envelope):
    f32 = jnp.float32
    bf16 = jnp.bfloat16
    crossed = crossed.transpose(1, 2, 0, 3).reshape(QX * QY, 2, ORDER * ORDER)
    bubble = bubble.transpose(0, 1, 3, 4, 2).reshape(QX * QY, NFF, NFF, NFREQ)
    bond_shift = bond_shift.transpose(0, 1, 3, 2)
    operands = [
        crossed, spread_source(), merge_x(), pair_map, bond_shift, envelope, vertex, bubble, same_frequency(),
        turn_columns(), y_forward(), rolled_rows(), x_back(), y_back(), split_x(), gather_rows(),
    ]
    operands = [jnp.asarray(operand) for operand in operands]
    hbm = pl.BlockSpec(memory_space=pl.ANY)
    result = pl.pallas_call(
        main_kernel,
        out_shape=jax.ShapeDtypeStruct(vertex.shape, bf16),
        in_specs=[hbm] * len(operands),
        out_specs=pl.BlockSpec(memory_space=pltpu.VMEM),
        scratch_shapes=[
            (pltpu.SMEM if array.dtype == jnp.int32 else pltpu.VMEM)(array.shape, array.dtype)
            for array in operands
        ] + [
            pltpu.VMEM((4, QX, 20 * NFREQ, 128), f32),
            pltpu.VMEM((DEVICES, SEND_ROWS, 128), bf16),
            pltpu.VMEM((DEVICES, SEND_ROWS, 128), bf16),
            pltpu.VMEM((4, 25 * LAT, 128), f32),
            pltpu.VMEM((2, 25 * NX * 8, 128), f32),
            pltpu.VMEM((DEVICES, BACK_ROWS, 128), bf16),
            pltpu.VMEM((DEVICES, BACK_ROWS, 128), bf16),
            pltpu.VMEM((2, LAT, 128), f32),
            pltpu.VMEM((80 * ORDER, 128), f32),
            pltpu.VMEM((250, 8, 128), f32),
            pltpu.VMEM((250, 128), f32),
            pltpu.VMEM((QX * QY * ORDER, 128), f32),
            pltpu.VMEM((QX * QY, ORDER, 128), bf16),
            pltpu.VMEM((QX, 192, 512), bf16),
            pltpu.VMEM((5, 192 * QX, 128), f32),
            pltpu.VMEM((80 * ORDER, 128), f32),
            pltpu.SemaphoreType.DMA((len(operands),)),
            pltpu.SemaphoreType.DMA,
            pltpu.SemaphoreType.DMA((NX,)),
            pltpu.SemaphoreType.DMA,
            pltpu.SemaphoreType.DMA((4,)),
        ],
        compiler_params=pltpu.CompilerParams(
            collective_id=0, has_side_effects=True, vmem_limit_bytes=60 * 2**20
        ),
    )(*operands)
    return result


def solution(mesh):
    placed = (
        P(None, "kx", "ky", None),
        P("kx", "ky", None),
        P("kx", "ky", None, None, None),
        P(),
        P(),
        P(),
    )
    return jax.shard_map(
        local, mesh=mesh, in_specs=placed, out_specs=P("kx", "ky", None), check_vma=False
    )
```

```python
import math

import jax
import jax.numpy as jnp
import ml_dtypes
import numpy as np
from jax import lax
from jax.experimental import pallas as pl
from jax.experimental.pallas import tpu as pltpu
from jax.sharding import PartitionSpec as P

LAT = 80
NFF = 5
NFREQ = 16
ORDER = 80
NX = 16
NY = 8
DEVICES = NX * NY
QX = LAT // NX
QY = LAT // NY
REACH = 2
SEND_ROWS = 40
BACK_ROWS = 24
BATCH = 25
BF16 = ml_dtypes.bfloat16
MESH = pl.DeviceIdType.MESH


def cas_table(count):
    phases = np.outer(np.arange(count), np.arange(count)) % count
    angles = phases * (2.0 * math.pi / count)
    return ((np.cos(angles) + np.sin(angles)) / math.sqrt(count)).astype(np.float32)


CAS = cas_table(LAT)


def rolled_rows():
    rows = (np.arange(LAT)[None, :] + np.arange(-REACH, REACH + 1)[:, None]) % LAT
    return CAS[rows].astype(BF16)


def y_forward():
    reach = np.zeros((LAT, 128), np.float32)
    columns = np.arange(LAT + 2 * REACH)
    reach[:, columns] = CAS[:, (columns - REACH) % LAT]
    reach = reach.reshape(NY, QY, 128)
    table = np.zeros((NY, 2, QY, 2, 2, 2, 128), np.float32)
    for chan in range(2):
        for half in range(2):
            table[:, half, :, chan, chan, half] = reach
    return table.reshape(NY * SEND_ROWS, 4 * 128).astype(BF16)


def x_back():
    table = np.zeros((NX, 8, LAT), np.float32)
    table[:, :QX] = CAS.reshape(NX, QX, LAT)
    return table.reshape(NX * 8, LAT).astype(BF16)


def y_back():
    table = np.zeros((NY, 2, 12, 2, 128), np.float32)
    for half in range(2):
        table[:, half, :QY, half, :LAT] = CAS.reshape(NY, QY, LAT)
    return table.reshape(NY * BACK_ROWS, 2 * 128).astype(BF16)


def spread_source():
    table = np.zeros((112 + 400 + 112, 16 * 32), np.float32)
    a, n2, b = np.meshgrid(np.arange(5), np.arange(16), np.arange(5), indexing="ij")
    table[112 + 80 * a + 5 * n2 + b, 32 * n2 + 5 * a + b] = 1
    return table.astype(BF16)


def merge_x():
    table = np.zeros((5, 4, 32, 4, 128), np.float32)
    qx, g, pair = np.meshgrid(np.arange(5), np.arange(4), np.arange(25), indexing="ij")
    table[qx, g, pair, g, 25 * qx + pair] = 1
    return table.reshape(640, 512).astype(BF16)


def split_x():
    return np.ascontiguousarray(merge_x().T)


def gather_rows():
    table = np.zeros((16, 32, 5, 128), np.float32)
    a, n2, b = np.meshgrid(np.arange(5), np.arange(16), np.arange(5), indexing="ij")
    table[n2, 5 * a + b, a, 5 * n2 + b] = 1
    return table.reshape(512, 640).astype(BF16)


def turn_columns():
    table = np.zeros((80, 128), np.float32)
    n, a = np.meshgrid(np.arange(16), np.arange(5), indexing="ij")
    table[5 * n + a, 16 * a + n] = 1
    return table.astype(BF16)


def same_frequency():
    table = np.zeros((16, 128), np.float32)
    n, b = np.meshgrid(np.arange(16), np.arange(5), indexing="ij")
    table[n, 16 * b + n] = 1
    return table


def partner_order():
    offsets = [(z, y, x, c) for z in range(4) for y in range(4) for x in range(4) for c in range(2)]
    offsets = [offset for offset in offsets if offset != (0, 0, 0, 0)]
    draw = np.random.RandomState(1).permutation(len(offsets))
    links = [sum(min(step, 4 - step) for step in offset[:3]) for offset in offsets]
    return [offsets[k] for k in sorted(range(len(offsets)), key=lambda k: (-links[k], draw[k]))]


def partners(mx, my):
    mz, my_y = mx // 4, my // 2
    mine_x = lax.rem(my, 2) * 2 + lax.rem(mx // 2, 2)
    mine_core = lax.rem(mx, 2)
    for z, y, x, core in partner_order():
        there = lax.rem(mine_x + x, 4)
        kx = lax.rem(mz + z, 4) * 4 + lax.rem(there, 2) * 2 + lax.rem(mine_core + core, 2)
        ky = lax.rem(my_y + y, 4) * 2 + there // 2
        yield kx, ky


def f32dot(left, right, dims=((1,), (0,))):
    return lax.dot_general(left, right, (dims, ((), ())), preferred_element_type=jnp.float32)


def build_slabs(crossed_ref, spread_ref, merge_ref, mixed_ref, slabs_ref):
    for n in range(NFREQ):
        start = 400 * n // 128 * 128
        offset = 400 * n - start
        rows = crossed_ref[:, :, start : start + 512].reshape(2 * QX * QY, 512)
        spread = f32dot(rows, spread_ref[112 - offset : 624 - offset, :])
        for part in range(4):
            for qx in range(QX):
                mixed_ref[part, qx, 20 * n : 20 * n + 20, :] = spread[
                    20 * qx : 20 * qx + 20, 128 * part : 128 * part + 128
                ]

    def one_part(part, carry):
        rows = jnp.concatenate([mixed_ref[part, qx] for qx in range(QX)], axis=1).astype(jnp.bfloat16)
        merged = f32dot(rows, merge_ref[...]).astype(jnp.bfloat16)
        for g in range(4):
            for pair in range(8):
                slabs_ref[(4 * part + g) * 8 + pair] = merged[
                    40 * pair : 40 * pair + 40, 128 * g : 128 * g + 128
                ]
        return carry

    for part in range(4):
        one_part(part, 0)


def prepare_vertex(
    vertex_ref, bubble_ref, turn_ref, same_ref, rows_ref, wide_ref, lines_ref, left_ref, right_ref
):
    for qx in range(QX):
        for i in range(ORDER):
            rows_ref[80 * i + 16 * qx : 80 * i + 16 * qx + 10, :80] = vertex_ref[
                qx, :, 80 * i : 80 * i + 80
            ].astype(jnp.float32)
    same = same_ref[...]
    wide_ref[:, :5, :16] = bubble_ref[...].reshape(250, 5, 16).astype(jnp.float32)
    lines_ref[:, :80] = jnp.concatenate([wide_ref[:, b, :16] for b in range(5)], axis=1)

    for start in range(0, QX * QY, BATCH):
        batch = range(start, start + BATCH)
        blocks = []
        bubbles = []
        for q in batch:
            at = q + 6 * (q // 10)
            blocks.append(
                jnp.concatenate(
                    [rows_ref[pl.ds(80 * a + at, 16, stride=400), :] for a in range(5)], axis=0
                ).astype(jnp.bfloat16)
            )
            bubbles.append(
                jnp.concatenate(
                    [lines_ref[pl.ds(5 * q + a, 1), :] * same for a in range(5)], axis=0
                ).astype(jnp.bfloat16)
            )
        turned = [f32dot(block[:, :80], turn_ref[...]).astype(jnp.bfloat16) for block in blocks]
        for q, block, bubble in zip(batch, blocks, bubbles):
            left = f32dot(bubble[:, :80], block)
            for a in range(5):
                left_ref[pl.ds(80 * q + a, 16, stride=5), :] = left[16 * a : 16 * a + 16]
        for q, bubble, matrix in zip(batch, bubbles, turned):
            right_ref[q] = f32dot(matrix[:, :80], bubble).astype(jnp.bfloat16)


def finish_part(part, got_ref, split_ref, spread_ref):
    rows = jnp.concatenate(
        [got_ref[8 * (4 * part + g) : 8 * (4 * part + g) + 8].reshape(192, 128) for g in range(4)], axis=1
    )
    apart = f32dot(rows, split_ref[...]).astype(jnp.bfloat16)
    for qx in range(QX):
        spread_ref[qx, :, 128 * part : 128 * part + 128] = apart[:, 128 * qx : 128 * qx + 128]


def finish(gather_ref, spread_ref, blocks_ref, left_ref, right_ref, rows_ref, out_ref):
    for qx in range(QX):
        found = f32dot(spread_ref[qx], gather_ref[...])
        for a in range(5):
            blocks_ref[a, 192 * qx : 192 * qx + 192, :] = found[:, 128 * a : 128 * a + 128]

    for q in range(QX * QY):
        at = q + 182 * (q // 10)
        block = jnp.concatenate(
            [blocks_ref[a, pl.ds(at, 16, stride=12), :] for a in range(5)], axis=0
        ).astype(jnp.bfloat16)
        left = left_ref[80 * q : 80 * q + 80, :].astype(jnp.bfloat16)
        result = f32dot(block[:, :80], left) + f32dot(right_ref[q][:, :80], block)
        put = q + 6 * (q // 10)
        for a in range(5):
            rows_ref[pl.ds(80 * a + put, 16, stride=400), :] = result[16 * a : 16 * a + 16]

    for qx in range(QX):
        for i in range(0, ORDER, 8):
            wide = jnp.concatenate(
                [rows_ref[80 * (i + k) + 16 * qx : 80 * (i + k) + 16 * qx + 16, :80] for k in range(8)], axis=1
            ).astype(jnp.bfloat16)
            out_ref[qx, :, 80 * i : 80 * i + 640] = wide[:10]


def main_kernel(*refs):
    (
        crossed_hbm, spread_hbm, merge_hbm, pair_hbm, shift_hbm, envelope_hbm, vertex_hbm, bubble_hbm, same_hbm,
        turn_hbm, yf_hbm, cas_hbm, xb_hbm, yb_hbm, split_hbm, gather_hbm,
        out_ref,
        crossed_ref, spread_ref, merge_ref, pair_ref, shift_ref, envelope_ref, vertex_ref, bubble_ref, same_ref,
        turn_ref, yf_ref, cas_ref, xb_ref, yb_ref, split_ref, gather_ref,
        mixed_ref, slabs_ref, recv_ref, half_ref, back_ref, outgoing_ref, got_ref, weight_ref,
        vertex_rows_ref, wide_ref, lines_ref, left_ref, right_ref, spread_back_ref, blocks_ref, out_rows_ref,
        load_sems, send_sem, recv_sems, back_send_sem, back_sems,
    ) = refs
    loads = [pltpu.make_async_copy(refs[k], refs[17 + k], load_sems.at[k]) for k in range(16)]
    for load in loads:
        load.start()
    mx = lax.axis_index("kx")
    my = lax.axis_index("ky")
    me = mx * NY + my
    barrier = pltpu.get_barrier_semaphore()

    for kx, ky in partners(mx, my):
        pl.semaphore_signal(barrier, inc=1, device_id=(kx, ky), device_id_type=MESH)
    for load in loads[:3]:
        load.wait()
    build_slabs(crossed_ref, spread_ref, merge_ref, mixed_ref, slabs_ref)
    own = pltpu.make_async_copy(slabs_ref.at[me], recv_ref.at[me], recv_sems.at[mx])
    own.start()
    pl.semaphore_wait(barrier, DEVICES - 1)

    for kx, ky in partners(mx, my):
        pltpu.make_async_remote_copy(
            src_ref=slabs_ref.at[kx * NY + ky],
            dst_ref=recv_ref.at[me],
            send_sem=send_sem,
            recv_sem=recv_sems.at[mx],
            device_id=(kx, ky),
            device_id_type=MESH,
        ).start()

    for load in loads[3:]:
        load.wait()
    weight_ref[...] = jnp.zeros_like(weight_ref)
    weight_ref[:, :, :LAT] = envelope_ref[...]
    prepare_vertex(
        vertex_ref, bubble_ref, turn_ref, same_ref, vertex_rows_ref, wide_ref, lines_ref, left_ref, right_ref
    )

    for group in range(NX):
        here = pl.ds(NY * group, NY)
        pltpu.make_async_copy(slabs_ref.at[here], recv_ref.at[here], recv_sems.at[group]).wait()
        block = recv_ref[here].reshape(NY * SEND_ROWS, 128)
        turned = f32dot(block, yf_ref[...], ((0,), (0,)))
        for part in range(4):
            half_ref[part, 125 * group : 125 * group + 125, :] = turned[:125, 128 * part : 128 * part + 128]

    reals = []
    for pair in range(25):
        for chan in range(2):
            rows = pl.ds(pair_ref[chan, pair], LAT, stride=25)
            operand = jnp.concatenate(
                [half_ref[2 * chan + half, rows, :] for half in range(2)], axis=1
            ).astype(jnp.bfloat16)
            step_x = shift_ref[chan, pair // 5, 0, pair % 5]
            reals.append(f32dot(cas_ref[step_x + REACH], operand))
    projected = []
    for pair in range(25):
        total = [None, None]
        for chan in range(2):
            step_y = shift_ref[chan, pair // 5, 1, pair % 5]
            for half in range(2):
                piece = reals[2 * pair + chan][:, 128 * half : 128 * half + 128]
                term = pltpu.roll(piece, 128 - REACH - step_y, 1) * weight_ref[chan]
                total[half] = term if chan == 0 else total[half] + term
        projected.append(jnp.concatenate(total, axis=1).astype(jnp.bfloat16))
    for pair in range(25):
        back = f32dot(xb_ref[...], projected[pair])
        for half in range(2):
            back_ref[half, pl.ds(pair, 128, stride=25), :] = back[:, 128 * half : 128 * half + 128]

    for group in range(NX):
        rows = pl.ds(200 * group, 128)
        operand = jnp.concatenate(
            [back_ref[half, rows, :] for half in range(2)], axis=1
        ).astype(jnp.bfloat16)
        result = f32dot(yb_ref[...], operand, ((1,), (1,))).astype(jnp.bfloat16)
        for lane in range(NY):
            outgoing_ref[NY * group + lane] = result[BACK_ROWS * lane : BACK_ROWS * lane + BACK_ROWS]
    pltpu.make_async_copy(outgoing_ref.at[me], got_ref.at[me], back_sems.at[mx // 4]).start()
    for kx, ky in partners(mx, my):
        pltpu.make_async_remote_copy(
            src_ref=outgoing_ref.at[kx * NY + ky],
            dst_ref=got_ref.at[me],
            send_sem=back_send_sem,
            recv_sem=back_sems.at[mx // 4],
            device_id=(kx, ky),
            device_id_type=MESH,
        ).start()

    most = pl.ds(0, DEVICES - 1)
    pltpu.make_async_copy(slabs_ref.at[most], recv_ref.at[most], send_sem).wait()
    for part in range(4):
        here = pl.ds(32 * part, 32)
        pltpu.make_async_copy(outgoing_ref.at[here], got_ref.at[here], back_sems.at[part]).wait()
        finish_part(part, got_ref, split_ref, spread_back_ref)
    finish(gather_ref, spread_back_ref, blocks_ref, left_ref, right_ref, out_rows_ref, out_ref)
    pltpu.make_async_copy(outgoing_ref.at[most], got_ref.at[most], back_send_sem).wait()


def local(crossed, vertex, bubble, pair_map, bond_shift, envelope):
    f32 = jnp.float32
    bf16 = jnp.bfloat16
    crossed = crossed.transpose(1, 2, 0, 3).reshape(QX * QY, 2, ORDER * ORDER)
    bubble = bubble.transpose(0, 1, 3, 4, 2).reshape(QX * QY, NFF, NFF, NFREQ)
    bond_shift = bond_shift.transpose(0, 1, 3, 2)
    operands = [
        crossed, spread_source(), merge_x(), pair_map, bond_shift, envelope, vertex, bubble, same_frequency(),
        turn_columns(), y_forward(), rolled_rows(), x_back(), y_back(), split_x(), gather_rows(),
    ]
    operands = [jnp.asarray(operand) for operand in operands]
    hbm = pl.BlockSpec(memory_space=pl.ANY)
    result = pl.pallas_call(
        main_kernel,
        out_shape=jax.ShapeDtypeStruct(vertex.shape, bf16),
        in_specs=[hbm] * len(operands),
        out_specs=pl.BlockSpec(memory_space=pltpu.VMEM),
        scratch_shapes=[
            (pltpu.SMEM if array.dtype == jnp.int32 else pltpu.VMEM)(array.shape, array.dtype)
            for array in operands
        ] + [
            pltpu.VMEM((4, QX, 20 * NFREQ, 128), f32),
            pltpu.VMEM((DEVICES, SEND_ROWS, 128), bf16),
            pltpu.VMEM((DEVICES, SEND_ROWS, 128), bf16),
            pltpu.VMEM((4, 25 * LAT + 32, 128), f32),
            pltpu.VMEM((2, 25 * NX * 8, 128), f32),
            pltpu.VMEM((DEVICES, BACK_ROWS, 128), bf16),
            pltpu.VMEM((DEVICES, BACK_ROWS, 128), bf16),
            pltpu.VMEM((2, LAT, 128), f32),
            pltpu.VMEM((80 * ORDER, 128), f32),
            pltpu.VMEM((250, 8, 128), f32),
            pltpu.VMEM((250, 128), f32),
            pltpu.VMEM((QX * QY * ORDER, 128), f32),
            pltpu.VMEM((QX * QY, ORDER, 128), bf16),
            pltpu.VMEM((QX, 192, 512), bf16),
            pltpu.VMEM((5, 192 * QX, 128), f32),
            pltpu.VMEM((80 * ORDER, 128), f32),
            pltpu.SemaphoreType.DMA((len(operands),)),
            pltpu.SemaphoreType.DMA,
            pltpu.SemaphoreType.DMA((NX,)),
            pltpu.SemaphoreType.DMA,
            pltpu.SemaphoreType.DMA((4,)),
        ],
        compiler_params=pltpu.CompilerParams(
            collective_id=0, has_side_effects=True, vmem_limit_bytes=60 * 2**20
        ),
    )(*operands)
    return result


def solution(mesh):
    placed = (
        P(None, "kx", "ky", None),
        P("kx", "ky", None),
        P("kx", "ky", None, None, None),
        P(),
        P(),
        P(),
    )
    return jax.shard_map(
        local, mesh=mesh, in_specs=placed, out_specs=P("kx", "ky", None), check_vma=False
    )
```
